256 devices in a mesh: grp: 2 (over y_hi), ep: 128 (over z, x, y_lo, core).
Axes of the slice: x: 4, y: 4 (y_hi: 2, y_lo: 2; y = y_hi * 2 + y_lo), z: 8, core: 2. Of those that a mesh axis runs over, the one named last changes fastest.
Arguments:
- rows_in: bfloat16 [1024, 7168], P(('grp', 'ep')), may hold values from -6 to 6
- expert_ids: int32 [1024, 8], P(('grp', 'ep')), may hold values from 0 to 15, all different within a row; in each aligned block of 4 rows (0 to 3, 4 to 7, ...) at most 3 rows name the same one
- gate_values: bfloat16 [1024, 8], P(('grp', 'ep')), may hold values from 0.049804688 to 0.5
- w_gate: bfloat16 [7168, 16384], P(None, 'ep'), may hold values from -0.0625 to 0.0625
- w_up: bfloat16 [7168, 16384], P(None, 'ep'), may hold values from -0.0625 to 0.0625
- w_down: bfloat16 [16384, 7168], P('ep'), may hold values from -0.1875 to 0.1875
- queries: bfloat16 [1024, 128, 576], P(('grp', 'ep')), may hold values from -24 to 24
- query_ids: int32 [1024], P(('grp', 'ep')), may hold values from 0 to 131, as said below
- latent_pool: bfloat16 [1048576, 576], P(('grp', 'ep')), may hold values from -4 to 4
- key_owner: int32 [1048576], P(('grp', 'ep')), may hold values from 0 to 3, as said below
- sent_pages: bfloat16 [8192, 576], P(('grp', 'ep')), may hold values from -4 to 4
- sent_length: int32 [256], P(('grp', 'ep')), may hold values from 1 to 32
- sent_rank: int32 [256], P(('grp', 'ep')), may hold values from 0 to 63, as said below
Outputs:
- expert_out: bfloat16 [1024, 7168], P(('grp', 'ep'))
- attention: bfloat16 [1024, 128, 512], P(('grp', 'ep'))
The draws below stay inside these ranges and needn't reach their ends.
Inputs may be any that keep to these rules, and one draw needn't show every extreme that they name: `expert_ids`: within the 4 rows of one device no expert is named by more than 3 rows; each row names distinct experts. On every device key_owner never falls, every request 0 to 3 owns one key or more, and request 0 owns the first 2048 keys. `query_ids`: A query id below 4 names a request of the row's own device; the last query row of every device belongs to request 0. An id 4 + s appears only on decode device sent_rank[s], in one of its first 2 rows, for every prefill device s exactly once. `sent_rank`: each decode device is chosen by at most 2 prefill devices.
All inputs are finite; a program needn't handle non-finite values.
Results may differ from the reference program's by a relative error of at most 0.0049.
Values may be sent and summed in bfloat16 or wider, within the bound.
No kernel may reach another device: no remote copies, remote signals or barrier semaphores. Data moves between devices by JAX's collectives and lax.ppermute only.
A program may use at most 128 MiB of HBM per device.

```python
import math
import jax
import jax.numpy as jnp
import numpy as np
from jax import lax

D = 7168
FF = 1024
EXPERTS = 16
TOPK = 8
HEADS = 128
LAT = 576
KVR = 512
ROWS = 4
KEYS = 4096
RES = 4
NEWLEN = 32
NEWMAX = 2
MOST = 3
TOKENS = 1024
SENT = 8192
N_EP = 128


def routing_order(key):
    return jax.random.permutation(jax.random.fold_in(key, 101), N_EP).astype(jnp.int32)


def anchor_rows(key):
    return jnp.clip(jax.random.normal(jax.random.fold_in(key, 103), (2 * N_EP, LAT), jnp.float32), -4.0, 4.0)


def draw_query_ids(key, part):
    ordering = routing_order(key)
    inverse = jnp.argsort(ordering).astype(jnp.int32)
    key = jax.random.fold_in(key, 3)
    resident = jax.random.randint(key, (2 * N_EP, ROWS), 0, RES).astype(jnp.int32)
    resident = resident.at[:, ROWS - 1].set(0)
    dest_iota = jnp.arange(N_EP, dtype=jnp.int32)[:, None]
    row_iota = jnp.arange(ROWS, dtype=jnp.int32)[None, :]
    slot_index = dest_iota * NEWMAX + row_iota
    arrival = (row_iota < NEWMAX) & (slot_index < N_EP)
    newcomer = RES + inverse[jnp.clip(slot_index, 0, N_EP - 1)]
    decode_rows = jnp.where(arrival, newcomer, resident[N_EP:])
    return jnp.concatenate([resident[:N_EP], decode_rows], axis=0).reshape(-1).astype(jnp.int32)


def draw_sent_rank(key, part):
    ordering = routing_order(key)
    key = jax.random.fold_in(key, 5)
    decode_order = jax.random.permutation(key, N_EP).astype(jnp.int32)
    return (jnp.concatenate([ordering, decode_order]) // NEWMAX).astype(jnp.int32)


def draw_sent_length(key, part):
    key = jax.random.fold_in(key, 7)
    lengths = jax.random.randint(key, (2 * N_EP,), 1, NEWLEN + 1).astype(jnp.int32)
    return lengths.at[0].set(NEWLEN)


def draw_key_owner(key, part):
    key = jax.random.fold_in(key, 9)
    half_keys = KEYS // 2
    device_keys = jax.random.split(key, 2 * N_EP)

    def cuts_for(one_key):
        chosen_cuts = jax.random.permutation(one_key, half_keys - 1)[:RES - 2].astype(jnp.int32)
        return jnp.concatenate([jnp.full((1,), half_keys, jnp.int32), jnp.sort(chosen_cuts) + half_keys + 1])
    boundaries = jax.vmap(cuts_for)(device_keys)
    positions = jnp.arange(KEYS, dtype=jnp.int32)
    owners = jnp.sum((positions[None, :, None] >= boundaries[:, None, :]).astype(jnp.int32), axis=-1)
    return owners.reshape(-1).astype(jnp.int32)


def draw_latent_pool(key, part):
    anchor = anchor_rows(key)
    key = jax.random.fold_in(key, 11)
    values = jnp.clip(jax.random.normal(key, (2 * N_EP, KEYS, LAT), jnp.float32), -4.0, 4.0)
    values = values.at[:, 0, :].set(anchor)
    return values.reshape(2 * N_EP * KEYS, LAT).astype(jnp.bfloat16)


def draw_queries(key, part):
    key = jax.random.fold_in(key, 13)
    values = jnp.clip(jax.random.normal(key, (2 * N_EP, ROWS, HEADS, LAT), jnp.float32), -4.0, 4.0)
    return values.reshape(2 * N_EP * ROWS, HEADS, LAT).astype(jnp.bfloat16)


def levels(rng, shape, cuts, smallest, top_value):
    factor_of = 1.0
    for axis_at, blocks in cuts:
        steps = jax.random.uniform(jax.random.fold_in(jax.random.fold_in(rng, 6), axis_at), (blocks,), jnp.float32, smallest / len(cuts), top_value / len(cuts))
        factor_of = factor_of * jnp.repeat(jnp.exp(steps), shape[axis_at] // blocks).reshape((-1,) + (1,) * (len(shape) - 1 - axis_at))
    return factor_of


def routed_block(stream_key, own, number, rows, amount, top, reach, slope):
    order = jax.random.permutation(stream_key, amount)
    packed, ordinary = portions_of(amount, rows * top, reach, slope, True), portions_of(amount, rows * top, reach, slope, False)
    places = jnp.arange(amount)

    def named(sizes, offset_by):
        used = int((sizes > 0).sum())
        fixed = max(1, used // 4)
        moved = fixed + (places - fixed + offset_by * (used - fixed)) % max(1, amount - fixed)
        return jnp.zeros((amount,), jnp.int32).at[order[jnp.where(places < fixed, places, moved)]].set(jnp.asarray(sizes, jnp.int32))

    sizes = jnp.where(number % 4 == 0, named(packed, number // 4), named(ordinary, number - number // 4 - 1))
    mixed = jax.random.permutation(jax.random.fold_in(own, 3), amount)
    source_of, taker = mixed[0:amount // 2 * 2:2], mixed[1:amount // 2 * 2:2]
    slack = jnp.minimum(sizes[source_of] - 1, reach - sizes[taker]) // 2
    slack = jnp.where((source_of == order[0]) | (taker == order[0]) | (sizes[taker] == 0), 0, jnp.maximum(slack, 0))
    moved = jax.random.randint(jax.random.fold_in(own, 4), (amount // 2,), 0, 1 << 20) % (slack + 1)
    sizes = sizes.at[source_of].add(-moved).at[taker].add(moved)
    labels = jnp.searchsorted(jnp.cumsum(sizes), jnp.arange(rows * top), side="right").astype(jnp.int32)
    grid = labels.reshape(top, rows).T
    grid = grid[jax.random.permutation(jax.random.fold_in(own, 1), rows)]
    offset_by = jax.random.randint(jax.random.fold_in(own, 2), (rows, 1), 0, top)
    return jnp.take_along_axis(grid, (jnp.arange(top)[None, :] + offset_by) % top, axis=1)


def portions_of(amount, total, limit, slope, full):
    weights = [(1 << 20) // math.isqrt(rank ** slope) + 1 for rank in range(1, amount + 1)]
    largest = limit if full else min(limit, max(-(-total // amount), total * weights[0] // sum(weights)))
    least = 1 if total - largest >= amount - 1 else 0
    given, spare = [largest] + [least] * (amount - 1), total - largest - least * (amount - 1)
    while spare > 0:
        free = [i for i in range(1, amount) if given[i] < largest] or [i for i in range(1, amount) if given[i] < limit]
        mass, left = sum([weights[i] for i in free]), spare
        for i in free:
            addition = min(limit - given[i], max(1, left * weights[i] // mass), spare)
            given[i] = given[i] + addition
            spare = spare - addition
    return np.array(given)


def bell_draw(rng, shape, spread, reach, cuts=(), held_as=jnp.bfloat16):
    entries = spread * jax.random.normal(rng, shape, jnp.float32)
    if cuts:
        entries = entries * levels(rng, shape, cuts, -0.22, 0.18)
    return jnp.clip(entries, -reach, reach).astype(held_as)


def setup_inputs(seed: int = 0) -> dict:
    key_of = jax.random.split(jax.random.key(seed), 14)
    rows_in = bell_draw(key_of[0], (TOKENS, D), 1.0, 6.0, ((0, 256),))
    expert_ids_keys = jax.random.split(jax.random.fold_in(key_of[1], 1), TOKENS // ROWS)
    expert_ids_turns = jax.random.permutation(jax.random.fold_in(key_of[1], 3), TOKENS // ROWS)
    expert_ids = jax.vmap(lambda own, number: routed_block(jax.random.fold_in(key_of[1], 2), own, number, ROWS, EXPERTS, TOPK, MOST, 1))(expert_ids_keys, expert_ids_turns).reshape((TOKENS, TOPK))
    gate_values = jnp.clip(jnp.exp(math.log(0.5) - 2.306499 * jax.random.uniform(key_of[2], (TOKENS, TOPK), jnp.float32) ** levels(key_of[2], (TOKENS, TOPK), ((0, 256),), -0.2, 0.2)), 0.049804688, 0.5).astype(jnp.bfloat16)
    w_gate = bell_draw(key_of[3], (D, EXPERTS * FF), D ** -0.5, 0.0625, ((1, 128),))
    w_up = bell_draw(key_of[4], (D, EXPERTS * FF), D ** -0.5, 0.0625, ((1, 128),))
    w_down = bell_draw(key_of[5], (EXPERTS * FF, D), FF ** -0.5, 0.1875, ((0, 128),))
    queries = draw_queries(jax.random.fold_in(key_of[13], 71), 0)
    query_ids = draw_query_ids(jax.random.fold_in(key_of[13], 71), 0)
    latent_pool = draw_latent_pool(jax.random.fold_in(key_of[13], 71), 0)
    key_owner = draw_key_owner(jax.random.fold_in(key_of[13], 71), 0)
    sent_pages = bell_draw(key_of[10], (SENT, LAT), 1.0, 4.0, ((0, 256),))
    sent_length = draw_sent_length(jax.random.fold_in(key_of[13], 71), 0)
    sent_rank = draw_sent_rank(jax.random.fold_in(key_of[13], 71), 0)
    return dict(rows_in=rows_in, expert_ids=expert_ids, gate_values=gate_values, w_gate=w_gate, w_up=w_up, w_down=w_down, queries=queries, query_ids=query_ids, latent_pool=latent_pool, key_owner=key_owner, sent_pages=sent_pages, sent_length=sent_length, sent_rank=sent_rank)


score_scale = 192.0 ** -0.5


def softmax_pair(scores_pool, pool_mask, scores_new, new_mask):
    highest = jnp.maximum(jnp.max(jnp.where(pool_mask, scores_pool, -jnp.inf), axis=-1), jnp.max(jnp.where(new_mask, scores_new, -jnp.inf), axis=-1))
    exp_pool = jnp.where(pool_mask, jnp.exp(scores_pool - highest[..., None]), 0.0)
    exp_new = jnp.where(new_mask, jnp.exp(scores_new - highest[..., None]), 0.0)
    denominator = jnp.sum(exp_pool, axis=-1) + jnp.sum(exp_new, axis=-1)
    probs_pool = (exp_pool / denominator[..., None]).astype(jnp.bfloat16)
    probs_new = (exp_new / denominator[..., None]).astype(jnp.bfloat16)
    return probs_pool, probs_new


def reference(rows_in, expert_ids, gate_values, w_gate, w_up, w_down, queries, query_ids, latent_pool, key_owner, sent_pages, sent_length, sent_rank):
    token_total = rows_in.shape[0]
    expert_iota = jnp.arange(EXPERTS, dtype=jnp.int32)
    matches = expert_ids[:, :, None] == expert_iota[None, None, :]
    weight = jnp.sum(jnp.where(matches, gate_values.astype(jnp.float32)[:, :, None], 0.0), axis=1)

    def expert_step(accumulated, expert):
        start_col = (expert * FF).astype(jnp.int32)
        gate_cols = lax.dynamic_slice_in_dim(w_gate, start_col, FF, 1)
        up_cols = lax.dynamic_slice_in_dim(w_up, start_col, FF, 1)
        down_rows = lax.dynamic_slice_in_dim(w_down, start_col, FF, 0)
        gate_proj = jnp.dot(rows_in, gate_cols, preferred_element_type=jnp.float32)
        up_proj = jnp.dot(rows_in, up_cols, preferred_element_type=jnp.float32)
        hidden = (jax.nn.silu(gate_proj) * up_proj).astype(jnp.bfloat16)
        output = jnp.dot(hidden, down_rows, preferred_element_type=jnp.float32)
        column = lax.dynamic_slice_in_dim(weight, expert, 1, 1)
        return accumulated + column * output, None

    accumulated, _ = lax.scan(expert_step, jnp.zeros((token_total, D), jnp.float32), expert_iota)
    expert_out = accumulated.astype(jnp.bfloat16)

    device_total = 2 * N_EP
    query_blocks = queries.reshape(device_total, ROWS, HEADS, LAT)
    id_blocks = query_ids.reshape(device_total, ROWS)
    pool_blocks = latent_pool.reshape(device_total, KEYS, LAT)
    owner_blocks = key_owner.reshape(device_total, KEYS)
    page_blocks = sent_pages.reshape(device_total, NEWLEN, LAT)
    token_iota = jnp.arange(NEWLEN, dtype=jnp.int32)

    def one_device(device):
        query_f = query_blocks[device].astype(jnp.float32)
        row_ids = id_blocks[device]
        pool_f = pool_blocks[device].astype(jnp.float32)
        owners = owner_blocks[device]
        source = row_ids - RES
        arrived = (source >= 0) & (source < N_EP) & (device >= N_EP)
        source_clip = jnp.clip(source, 0, N_EP - 1).astype(jnp.int32)
        new_f = page_blocks[source_clip].astype(jnp.float32)
        new_valid = arrived[:, None] & (sent_rank[source_clip] == device - N_EP)[:, None] & (token_iota[None, :] < sent_length[source_clip][:, None])
        owner_match = row_ids[:, None] == owners[None, :]
        scores_pool = jnp.einsum('rhl,kl->rhk', query_f, pool_f) * score_scale
        scores_new = jnp.einsum('rhl,rnl->rhn', query_f, new_f) * score_scale
        probs_pool, probs_new = softmax_pair(scores_pool, owner_match[:, None, :], scores_new, new_valid[:, None, :])
        mixed = jnp.einsum('rhk,kv->rhv', probs_pool.astype(jnp.float32), pool_f[:, :KVR])
        mixed = mixed + jnp.einsum('rhn,rnv->rhv', probs_new.astype(jnp.float32), new_f[:, :, :KVR])
        return mixed.astype(jnp.bfloat16)

    attention = lax.map(one_device, jnp.arange(device_total, dtype=jnp.int32))
    return expert_out, attention.reshape(device_total * ROWS, HEADS, KVR)
```

```python
import jax
import jax.numpy as jnp
from jax import lax
from jax.sharding import Mesh, PartitionSpec as P

EXPERTS = 16
KVR = 512
RES = 4
NEWMAX = 2
NZ, NX, NY, NC = 8, 4, 2, 2
EP = ("z", "x", "y", "c")
ALL = ("g",) + EP
SUB = 2

score_scale = 192.0 ** (-0.5)


def shift(value, axis, by):
    length = lax.axis_size(axis)
    return lax.ppermute(value, axis, [(i, (i + by) % length) for i in range(length)])


def softmax_pair(scores_pool, pool_mask, scores_new, new_mask):
    highest = jnp.maximum(
        jnp.max(jnp.where(pool_mask, scores_pool, -jnp.inf), axis=-1),
        jnp.max(jnp.where(new_mask, scores_new, -jnp.inf), axis=-1),
    )
    exp_pool = jnp.where(pool_mask, jnp.exp(scores_pool - highest[..., None]), 0.0)
    exp_new = jnp.where(new_mask, jnp.exp(scores_new - highest[..., None]), 0.0)
    denominator = jnp.sum(exp_pool, axis=-1) + jnp.sum(exp_new, axis=-1)
    probs_pool = (exp_pool / denominator[..., None]).astype(jnp.bfloat16)
    probs_new = (exp_new / denominator[..., None]).astype(jnp.bfloat16)
    return (probs_pool, probs_new)


def handover(sent_pages, sent_length, sent_rank, weight_out):
    rank_count = weight_out.shape[0]
    new_len, latent_width = sent_pages.shape
    bf16 = jnp.bfloat16
    token_iota = jnp.arange(new_len, dtype=jnp.int32)
    rank_iota = jnp.arange(rank_count, dtype=jnp.int32)
    masked = jnp.where(token_iota[:, None] < sent_length[0], sent_pages, jnp.zeros_like(sent_pages))
    meta = jnp.concatenate([sent_length, sent_rank]).astype(bf16)
    meta = jnp.pad(meta, (0, latent_width - 2))[None]
    moved = lax.ppermute(jnp.concatenate([masked, meta]), "g", [(0, 1)])
    pieces = moved[:new_len].reshape(rank_count, -1)
    width = pieces.shape[1]
    meta = jnp.broadcast_to(moved[new_len:, :2], (rank_count, 2))
    out = jnp.concatenate([pieces, meta, weight_out], axis=1)
    arrived = lax.all_to_all(out, EP, split_axis=0, concat_axis=0, tiled=True)
    weight_in = arrived[:, width + 2 :]
    ranks_in = arrived[:, width + 1].astype(jnp.int32)
    same = ranks_in[:, None] == ranks_in[None, :]
    order_in = jnp.sum((same & (rank_iota[None, :] < rank_iota[:, None])).astype(jnp.int32), axis=1)
    slot_iota = jnp.arange(NEWMAX, dtype=jnp.int32)
    selected = (ranks_in[None, None, :] == rank_iota[:, None, None]) & (
        order_in[None, None, :] == slot_iota[None, :, None]
    )
    names = (rank_iota + 1).astype(bf16)[:, None]
    carried = jnp.concatenate([arrived[:, : width + 1], names], axis=1)
    buckets = jnp.einsum(
        "djs,sp->djp", selected.astype(bf16), carried, preferred_element_type=jnp.float32
    ).astype(bf16)
    got = lax.all_to_all(
        buckets.reshape(rank_count, -1), EP, split_axis=0, concat_axis=0, tiled=True
    ).reshape(rank_count, NEWMAX, width + 2)
    slot_pages = jnp.transpose(got[:, :, :width], (1, 0, 2)).reshape(NEWMAX, new_len, latent_width)
    slot_length = got[0, :, width].astype(jnp.int32)
    slot_source = got[0, :, width + 1].astype(jnp.int32) - 1
    return slot_pages, slot_source, slot_length, weight_in


def attend(queries, query_ids, latent_pool, key_owner, slot_pages, slot_source, slot_length):
    new_len = slot_pages.shape[1]
    token_iota = jnp.arange(new_len, dtype=jnp.int32)
    source = query_ids - RES
    arrived_new = source >= 0
    matching = arrived_new[:, None] & (source[:, None] == slot_source[None, :])
    new_keys = jnp.sum(
        jnp.where(matching[:, :, None, None], slot_pages[None].astype(jnp.float32), 0.0), axis=1
    ).astype(jnp.bfloat16)
    row_length = jnp.sum(jnp.where(matching, slot_length[None, :], 0), axis=1).astype(jnp.int32)
    new_valid = arrived_new[:, None] & (token_iota[None, :] < row_length[:, None])
    owner_match = query_ids[:, None] == key_owner[None, :]
    scores_pool = (
        jnp.einsum("rhl,kl->rhk", queries, latent_pool, preferred_element_type=jnp.float32)
        * score_scale
    )
    scores_new = (
        jnp.einsum("rhl,rnl->rhn", queries, new_keys, preferred_element_type=jnp.float32)
        * score_scale
    )
    probs_pool, probs_new = softmax_pair(
        scores_pool, owner_match[:, None, :], scores_new, new_valid[:, None, :]
    )
    mixed = jnp.einsum(
        "rhk,kv->rhv", probs_pool, latent_pool[:, :KVR], preferred_element_type=jnp.float32
    )
    mixed = mixed + jnp.einsum(
        "rhn,rnv->rhv", probs_new, new_keys[:, :, :KVR], preferred_element_type=jnp.float32
    )
    return mixed.astype(jnp.bfloat16)


def shards(
    rows_in,
    expert_ids,
    gate_values,
    w_gate,
    w_up,
    w_down,
    queries,
    query_ids,
    latent_pool,
    key_owner,
    sent_pages,
    sent_length,
    sent_rank,
):
    bf16, f32 = jnp.bfloat16, jnp.float32
    rows, width = rows_in.shape
    half = width // NC
    z, core = lax.axis_index("z"), lax.axis_index("c")
    rank_count = NZ * NX * NY * NC

    matches = expert_ids[:, :, None] == jnp.arange(EXPERTS, dtype=jnp.int32)[None, None, :]
    weight = jnp.sum(jnp.where(matches, gate_values.astype(f32)[:, :, None], 0.0), axis=1)
    weight_out = jnp.repeat(weight.T.astype(bf16), rank_count // EXPERTS, axis=0)

    def halves(value, axis):
        size = value.shape[axis] // NC
        mine = lax.dynamic_slice_in_dim(value, core * size, size, axis)
        theirs = lax.dynamic_slice_in_dim(value, (1 - core) * size, size, axis)
        return mine, shift(theirs, "c", 1)

    mine, other = halves(rows_in, 1)
    chip_rows = jnp.where(
        core == 0, jnp.concatenate([mine, other]), jnp.concatenate([other, mine])
    )
    plane = NX * NY
    block = plane * NC * rows
    spread = jnp.broadcast_to(chip_rows[None], (plane,) + chip_rows.shape).reshape(block, half)
    own = lax.all_to_all(spread, ("x", "y"), split_axis=0, concat_axis=0, tiled=True)

    gate_mine, gate_other = halves(w_gate, 0)
    up_mine, up_other = halves(w_up, 0)
    down_mine, down_other = halves(w_down, 1)
    w_in = jnp.concatenate([gate_mine, gate_other, up_mine, up_other], axis=1)
    w_out = jnp.concatenate([down_mine, down_other], axis=0)
    hid = w_gate.shape[1]

    slot_pages, slot_source, slot_length, weight_in = handover(
        sent_pages, sent_length, sent_rank, weight_out
    )
    weight_in = weight_in.reshape(NZ, block).astype(f32)

    parts = [own[:, i * half // SUB : (i + 1) * half // SUB] for i in range(SUB)]
    blocks = {0: parts}
    ahead, behind = list(parts), list(parts)
    for k in range(1, NZ // 2):
        ahead = [shift(p, "z", 1) for p in ahead]
        behind = [shift(p, "z", -1) for p in behind]
        blocks[-k] = ahead
        blocks[k] = behind
    far = NZ // 2
    blocks[far] = [shift(p, "z", 1 if i < SUB // 2 else -1) for i, p in enumerate(
        ahead[: SUB // 2] + behind[SUB // 2 :]
    )]

    def partials(offsets):
        data = [jnp.concatenate([blocks[o][i] for o in offsets]) for i in range(SUB)]
        size = half // SUB
        proj = sum(
            jnp.dot(data[i], w_in[i * size : (i + 1) * size], preferred_element_type=f32)
            for i in range(SUB)
        )
        came = shift(proj, "c", 1)
        swapped = jnp.concatenate(
            [came[:, hid : 2 * hid], came[:, :hid], came[:, 3 * hid :], came[:, 2 * hid : 3 * hid]],
            axis=1,
        )
        proj = proj + swapped
        hidden = (jax.nn.silu(proj[:, : 2 * hid]) * proj[:, 2 * hid :]).astype(bf16)
        result = jnp.dot(hidden, w_out, preferred_element_type=f32)
        found = {}
        for n, o in enumerate(offsets):
            scale = lax.dynamic_index_in_dim(weight_in, (z + o) % NZ, 0, keepdims=False)
            found[o] = result[n * block : (n + 1) * block] * scale[:, None]
        return found

    part = {}
    for offsets in ((0,), (-1, 1), (-2, 2), (-3, 3), (4,)):
        part.update(partials(offsets))

    def piece(o, i):
        return part[o][:, i * half // SUB : (i + 1) * half // SUB]

    totals = []
    for i in range(SUB):
        up = piece(far, i) if i < SUB // 2 else None
        down = piece(far, i) if i >= SUB // 2 else None
        for k in range(NZ // 2 - 1, -1, -1):
            if up is not None:
                up = shift(up.astype(bf16), "z", 1).astype(f32)
            if down is not None:
                down = shift(down.astype(bf16), "z", -1).astype(f32)
            if k:
                up = piece(k, i) if up is None else up + piece(k, i)
                down = piece(-k, i) if down is None else down + piece(-k, i)
        totals.append(piece(0, i) + up + down)
    total = jnp.concatenate(totals, axis=1).astype(bf16)
    total = lax.all_to_all(total, ("x", "y"), split_axis=0, concat_axis=0, tiled=True)
    total = jnp.sum(total.reshape(plane, NC * rows, half).astype(f32), axis=0).astype(bf16)
    mine = lax.dynamic_slice_in_dim(total, core * rows, rows, 0)
    other = shift(lax.dynamic_slice_in_dim(total, (1 - core) * rows, rows, 0), "c", 1)
    expert_out = jnp.where(
        core == 0,
        jnp.concatenate([mine, other], axis=1),
        jnp.concatenate([other, mine], axis=1),
    )

    attention = attend(
        queries, query_ids, latent_pool, key_owner, slot_pages, slot_source, slot_length
    )
    return (expert_out, attention)


def solution(mesh):
    fine = Mesh(mesh.devices.reshape(2, NZ, NX, NY, NC), ALL)
    placed = (
        P(ALL, None),
        P(ALL, None),
        P(ALL, None),
        P(None, EP),
        P(None, EP),
        P(EP, None),
        P(ALL, None, None),
        P(ALL),
        P(ALL, None),
        P(ALL),
        P(ALL, None),
        P(ALL),
        P(ALL),
    )
    return jax.shard_map(
        shards,
        mesh=fine,
        in_specs=placed,
        out_specs=(P(ALL, None), P(ALL, None, None)),
        check_vma=False,
    )
```

```python
import jax
import jax.numpy as jnp
from jax import lax
from jax.experimental import pallas as pl
from jax.experimental.pallas import tpu as pltpu
from jax.sharding import Mesh, PartitionSpec as P

EXPERTS = 16
KVR = 512
RES = 4
NEWMAX = 2
NZ, NX, NY, NC = 8, 4, 2, 2
EP = ("z", "x", "y", "c")
ALL = ("g",) + EP

score_scale = 192.0 ** (-0.5)


def shift(value, axis, by):
    length = lax.axis_size(axis)
    return lax.ppermute(value, axis, [(i, (i + by) % length) for i in range(length)])


def tie(*values):
    return lax.optimization_barrier(values)


def cached_kernel(ids_ref, owner_ref, q_ref, pool_ref, out_ref, score_ref):
    rows, _, heads = q_ref.shape
    keys = pool_ref.shape[1]
    step, lanes = 512, 128
    columns = [slice(n * lanes, (n + 1) * lanes) for n in range(step // lanes)]
    blocks = [slice(n, n + step) for n in range(0, keys, step)]
    queries = jnp.concatenate([q_ref[r] for r in range(rows)], axis=1).T
    tops = [jnp.full((heads, lanes), -jnp.inf, jnp.float32) for _ in range(rows)]
    for at in blocks:
        scores = jnp.dot(queries, pool_ref[:, at], preferred_element_type=jnp.float32)
        for r in range(rows):
            part = scores[r * heads : (r + 1) * heads] * score_scale
            part = jnp.where(owner_ref[:, at] == ids_ref[r], part, -jnp.inf)
            score_ref[r, :, at] = part
            for column in columns:
                tops[r] = jnp.maximum(tops[r], part[:, column])
    inverse = []
    for r in range(rows):
        top = jnp.maximum(jnp.max(tops[r], axis=1, keepdims=True), -3e38)
        total = jnp.zeros((heads, lanes), jnp.float32)
        for at in blocks:
            part = jnp.exp(score_ref[r, :, at] - top)
            score_ref[r, :, at] = part
            for column in columns:
                total = total + part[:, column]
        inverse.append(1.0 / jnp.maximum(jnp.sum(total, axis=1, keepdims=True), 1e-30))
    mixed = jnp.zeros((rows * heads, KVR), jnp.float32)
    for at in blocks:
        probs = [(score_ref[r, :, at] * inverse[r]).astype(jnp.bfloat16) for r in range(rows)]
        mixed = mixed + lax.dot_general(
            jnp.concatenate(probs),
            pool_ref[:KVR, at],
            (((1,), (1,)), ((), ())),
            preferred_element_type=jnp.float32,
        )
    out_ref[...] = mixed.reshape(out_ref.shape).astype(out_ref.dtype)


def attend_cached(queries, query_ids, latent_pool, key_owner):
    rows, heads, latent = queries.shape
    keys = latent_pool.shape[0]
    return pl.pallas_call(
        cached_kernel,
        out_shape=jax.ShapeDtypeStruct((rows, heads, KVR), jnp.bfloat16),
        in_specs=[pl.BlockSpec(memory_space=pltpu.SMEM)]
        + [pl.BlockSpec(memory_space=pltpu.VMEM)] * 3,
        out_specs=pl.BlockSpec(memory_space=pltpu.VMEM),
        scratch_shapes=[pltpu.VMEM((rows, heads, keys), jnp.float32)],
        compiler_params=pltpu.CompilerParams(vmem_limit_bytes=40 << 20),
        cost_estimate=pl.CostEstimate(
            flops=2 * rows * heads * keys * (latent + KVR),
            bytes_accessed=2 * keys * latent,
            transcendentals=rows * heads * keys,
        ),
    )(query_ids, key_owner.reshape(1, keys), jnp.swapaxes(queries, 1, 2), latent_pool.T)


def attend_new(queries, query_ids, pages, source_of, length_of):
    bf16, f32 = jnp.bfloat16, jnp.float32
    slots, new_len, latent_width = pages.shape
    token_iota = jnp.arange(new_len, dtype=jnp.int32)
    matching = query_ids[:, None] - RES == source_of[None, :]
    new_keys = jnp.dot(
        matching.astype(bf16), pages.reshape(slots, -1), preferred_element_type=f32
    ).astype(bf16)
    new_keys = new_keys.reshape(-1, new_len, latent_width)
    row_length = jnp.sum(jnp.where(matching, length_of[None, :], 0), axis=1)
    valid = (token_iota[None, :] < row_length[:, None])[:, None, :]
    scores = jnp.einsum("rhl,rnl->rhn", queries, new_keys, preferred_element_type=f32)
    scores = jnp.where(valid, scores * score_scale, -jnp.inf)
    weights = jnp.where(valid, jnp.exp(scores - jnp.max(scores, axis=-1, keepdims=True)), 0.0)
    probs = (weights / jnp.sum(weights, axis=-1, keepdims=True)).astype(bf16)
    return jnp.einsum("rhn,rnv->rhv", probs, new_keys[:, :, :KVR], preferred_element_type=f32)


def shards(
    rows_in,
    expert_ids,
    gate_values,
    w_gate,
    w_up,
    w_down,
    queries,
    query_ids,
    latent_pool,
    key_owner,
    sent_pages,
    sent_length,
    sent_rank,
):
    bf16, f32 = jnp.bfloat16, jnp.float32
    rows, width = rows_in.shape
    half = width // NC
    z, core = lax.axis_index("z"), lax.axis_index("c")
    place = lax.axis_index(("z", "x", "y", "c"))
    rank_count = NZ * NX * NY * NC
    plane = NX * NY
    block = plane * NC * rows
    new_len, latent_width = sent_pages.shape
    hid = w_gate.shape[1]

    def halves(value, axis):
        size = value.shape[axis] // NC
        mine = lax.dynamic_slice_in_dim(value, core * size, size, axis)
        theirs = lax.dynamic_slice_in_dim(value, (1 - core) * size, size, axis)
        return mine, shift(theirs, "c", 1)

    def in_order(mine, other, axis):
        return jnp.where(
            core == 0,
            jnp.concatenate([mine, other], axis=axis),
            jnp.concatenate([other, mine], axis=axis),
        )

    facts = jnp.concatenate([sent_length, sent_rank, place[None] + 1]).astype(bf16)
    facts = jnp.pad(facts[None], ((0, 0), (0, latent_width - 3)))
    moved = lax.ppermute(jnp.concatenate([sent_pages, facts]), "g", [(0, 1)])

    mine, other = halves(rows_in, 1)
    expert_iota = jnp.arange(EXPERTS, dtype=jnp.int32)
    matches = expert_ids[:, :, None] == expert_iota[None, None]
    weight = jnp.sum(jnp.where(matches, gate_values.astype(f32)[:, :, None], 0.0), axis=1)
    weight = weight.astype(bf16)
    expert_iota = expert_iota[None]
    chip_rows = in_order(mine, other, 0)
    chip_weight = in_order(weight, shift(weight, "c", 1), 0)

    wide = latent_width // 2
    piece = jnp.concatenate(
        [moved[:new_len, n * wide : (n + 1) * wide].reshape(plane, -1, wide) for n in range(2)],
        axis=1,
    )
    facts = jnp.broadcast_to(moved[new_len:, None, :3], (plane, NC * rows, 3))
    spread = jnp.concatenate(
        [
            jnp.broadcast_to(chip_rows[None], (plane,) + chip_rows.shape),
            piece,
            jnp.broadcast_to(chip_weight[None], (plane,) + chip_weight.shape),
            facts,
        ],
        axis=2,
    )
    used = spread.shape[2]
    spread = jnp.pad(spread, ((0, 0), (0, 0), (0, -used % 128))).reshape(block, -1)
    at_weight = half + wide
    at_facts = at_weight + EXPERTS - half

    spread, w_gate, w_up, w_down = tie(spread, w_gate, w_up, w_down)
    own = lax.all_to_all(spread, ("x", "y"), split_axis=0, concat_axis=0, tiled=True)

    gate_mine, gate_other = halves(w_gate, 0)
    up_mine, up_other = halves(w_up, 0)
    down_mine, down_other = halves(w_down, 1)
    w_in = jnp.concatenate([gate_mine, gate_other, up_mine, up_other], axis=1)
    w_out = jnp.concatenate([down_mine, down_other], axis=0)
    own, w_in, w_out = tie(own, w_in, w_out)

    expert = z * (EXPERTS // NZ) + lax.axis_index("x") // (NX * NZ // EXPERTS)

    def enter(*data):
        data = jnp.concatenate(data)
        proj = jnp.dot(data[:, :half], w_in, preferred_element_type=f32)
        scale = jnp.sum(
            jnp.where(
                expert_iota == expert, data[:, at_weight : at_weight + EXPERTS].astype(f32), 0.0
            ),
            axis=1,
            keepdims=True,
        )
        return proj, scale, shift(proj, "c", 1)

    def leave(proj, scale, came):
        swapped = jnp.concatenate(
            [came[:, hid : 2 * hid], came[:, :hid], came[:, 3 * hid :], came[:, 2 * hid : 3 * hid]],
            axis=1,
        )
        proj = proj + swapped
        hidden = (jax.nn.silu(proj[:, : 2 * hid]) * proj[:, 2 * hid :]).astype(bf16)
        result = jnp.dot(hidden, w_out, preferred_element_type=f32) * scale
        return [result[n : n + block // 2] for n in range(0, result.shape[0], block // 2)]

    def send(pair):
        return shift(pair[0], "z", 1), shift(pair[1], "z", -1)

    def after(pair, *others):
        tied = tie(*pair, *others)
        return tied[:2], *tied[2:]

    top, low = own[: block // 2], own[block // 2 :]
    lead, back = (top, low), (low, top)
    lead1, back1 = send(lead), send(back)
    proj0, scale0, came0 = enter(top, low)
    lead1, proj0, scale0, *_ = after(lead1, proj0, scale0, *back)
    lead2 = send(lead1)
    back1, came0, *_ = after(back1, came0, *lead1)
    back2 = send(back1)
    proj1, scale1, came1 = enter(*lead1, *back1)
    part0 = leave(proj0, scale0, came0)
    lead2, proj1, scale1, part0[0], part0[1], *_ = after(lead2, proj1, scale1, *part0, *back1)
    lead3 = send(lead2)
    back2, came1, *_ = after(back2, came1, *lead2)
    back3 = send(back2)
    proj2, scale2, came2 = enter(*lead2, *back2)
    lead3, proj2, scale2, came1, *_ = after(lead3, proj2, scale2, came1, *back2)
    lead4 = send(lead3)
    part1 = leave(proj1, scale1, came1)
    back3, came2, *tied = after(back3, came2, *part1, *lead3)
    part1 = tied[: len(part1)]
    proj3, scale3, came3 = enter(*lead3, *back3)
    part2 = leave(proj2, scale2, came2)
    lead4, proj3, scale3, *tied = after(lead4, proj3, scale3, *part2)
    part2 = tied
    proj4, scale4, came4 = enter(*lead4)
    proj4, came3 = tie(proj4, came3)
    part3 = leave(proj3, scale3, came3)
    part4 = leave(proj4, scale4, came4)

    pieces = jnp.concatenate(
        [p[:, half:] for p in (own, *lead1, *back1, *lead2, *back2, *lead3, *back3, *lead4)]
    )
    pieces = pieces.reshape(NZ * plane, NC * rows, -1)
    ranks = pieces[:, 0, at_facts + 1].astype(jnp.int32)
    source_iota = jnp.arange(NZ * plane, dtype=jnp.int32)
    same = ranks[:, None] == ranks[None, :]
    turn = jnp.sum((same & (source_iota[None, :] < source_iota[:, None])).astype(jnp.int32), axis=1)
    here = z * (plane * NC) + jnp.arange(plane * NC, dtype=jnp.int32)
    slot_iota = jnp.arange(NEWMAX, dtype=jnp.int32)
    selected = (ranks[None, None, :] == here[:, None, None]) & (
        turn[None, None, :] == slot_iota[None, :, None]
    )
    selected = selected.reshape(plane, NC * NEWMAX, NZ * plane).astype(bf16)

    def add(got, mine):
        return tuple((g.astype(f32) + m).astype(bf16) for g, m in zip(got, mine))

    lead = tie(*(p.astype(bf16) for p in part4))
    back = tie(part3[1].astype(bf16), part3[0].astype(bf16))
    ups = {3: (part3[3], part3[2]), 2: (part2[3], part2[2]), 1: (part1[3], part1[2])}
    rest = {2: (part2[1], part2[0]), 1: (part1[1], part1[0])}
    lead_got, back_got = send(lead), send(back)
    for k in (3, 2, 1):
        lead_got, *_ = after(lead_got, *back)
        lead = tie(*add(lead_got, ups[k]))
        lead_got = send(lead)
        if k > 1:
            back_got, *_ = after(back_got, *lead)
            back = tie(*add(back_got, rest[k - 1]))
            back_got = send(back)
        if k == 3:
            pieces, selected, *_ = tie(pieces, selected, *back)
            bound = jnp.einsum("pks,sij->pikj", selected, pieces, preferred_element_type=f32)
            bound = bound.astype(bf16).reshape(plane, NC * rows, NC, -1)
            mine = lax.dynamic_index_in_dim(bound, core, 2, keepdims=False)
            other = shift(lax.dynamic_index_in_dim(bound, 1 - core, 2, keepdims=False), "c", 1)
            bound = jnp.concatenate([mine, other], axis=2).reshape(block, -1)
        if k == 2:
            bound, *_ = tie(bound, *lead)
    total = jnp.concatenate(
        [
            part0[0] + lead_got[0].astype(f32) + back_got[1].astype(f32),
            part0[1] + back_got[0].astype(f32) + lead_got[1].astype(f32),
        ]
    ).astype(bf16)
    total = jnp.concatenate([total, bound], axis=1)
    total, queries, query_ids, latent_pool, key_owner = tie(
        total, queries, query_ids, latent_pool, key_owner
    )
    total = lax.all_to_all(total, ("x", "y"), split_axis=0, concat_axis=0, tiled=True)

    mixed = attend_cached(queries, query_ids, latent_pool, key_owner)
    total, mixed = tie(total, mixed)
    got = total[:, half:]
    total = jnp.sum(total[:, :half].reshape(plane, NC * rows, half).astype(f32), axis=0)
    total = total.astype(bf16)
    mine = lax.dynamic_slice_in_dim(total, core * rows, rows, 0)
    other = shift(lax.dynamic_slice_in_dim(total, (1 - core) * rows, rows, 0), "c", 1)
    expert_out = in_order(mine, other, 1)

    got = got.reshape(plane, 2, rows, NC * NEWMAX, -1)
    pages = jnp.concatenate([got[:, 0, :, :, :wide], got[:, 1, :, :, :wide]], axis=-1)
    pages = jnp.transpose(pages, (2, 0, 1, 3)).reshape(NC * NEWMAX, new_len, latent_width)
    facts = got[0, 0, 0, :, at_facts : at_facts + 3].astype(jnp.int32)
    mixed_new = attend_new(queries, query_ids, pages, facts[:, 2] - 1, facts[:, 0])
    attention = jnp.where(query_ids[:, None, None] >= RES, mixed_new.astype(bf16), mixed)
    return (expert_out, attention)


def solution(mesh):
    fine = Mesh(mesh.devices.reshape(2, NZ, NX, NY, NC), ALL)
    placed = (
        P(ALL, None),
        P(ALL, None),
        P(ALL, None),
        P(None, EP),
        P(None, EP),
        P(EP, None),
        P(ALL, None, None),
        P(ALL),
        P(ALL, None),
        P(ALL),
        P(ALL, None),
        P(ALL),
        P(ALL),
    )
    return jax.shard_map(
        shards,
        mesh=fine,
        in_specs=placed,
        out_specs=(P(ALL, None), P(ALL, None, None)),
        check_vma=False,
    )
```

```python
import jax
import jax.numpy as jnp
from jax import lax
from jax.experimental import pallas as pl
from jax.experimental.pallas import tpu as pltpu
from jax.sharding import Mesh, PartitionSpec as P

EXPERTS = 16
KVR = 512
RES = 4
NEWMAX = 2
NZ, NX, NY, NC = 8, 4, 2, 2
EP = ("z", "x", "y", "c")
ALL = ("g",) + EP

score_scale = 192.0 ** (-0.5)


def shift(value, axis, by):
    length = lax.axis_size(axis)
    return lax.ppermute(value, axis, [(i, (i + by) % length) for i in range(length)])


def tie(*values):
    return lax.optimization_barrier(values)


def cached_kernel(ids_ref, owner_ref, q_ref, pool_ref, out_ref, score_ref):
    rows, _, heads = q_ref.shape
    keys = pool_ref.shape[1]
    step, lanes = 512, 128
    columns = [slice(n * lanes, (n + 1) * lanes) for n in range(step // lanes)]
    blocks = [slice(n, n + step) for n in range(0, keys, step)]
    queries = jnp.concatenate([q_ref[r] for r in range(rows)], axis=1).T
    tops = [jnp.full((heads, lanes), -jnp.inf, jnp.float32) for _ in range(rows)]
    for at in blocks:
        scores = jnp.dot(queries, pool_ref[:, at], preferred_element_type=jnp.float32)
        for r in range(rows):
            part = scores[r * heads : (r + 1) * heads] * score_scale
            part = jnp.where(owner_ref[:, at] == ids_ref[r], part, -jnp.inf)
            score_ref[r, :, at] = part
            for column in columns:
                tops[r] = jnp.maximum(tops[r], part[:, column])
    inverse = []
    for r in range(rows):
        top = jnp.maximum(jnp.max(tops[r], axis=1, keepdims=True), -3e38)
        total = jnp.zeros((heads, lanes), jnp.float32)
        for at in blocks:
            part = jnp.exp(score_ref[r, :, at] - top)
            score_ref[r, :, at] = part
            for column in columns:
                total = total + part[:, column]
        inverse.append(1.0 / jnp.maximum(jnp.sum(total, axis=1, keepdims=True), 1e-30))
    mixed = jnp.zeros((rows * heads, KVR), jnp.float32)
    for at in blocks:
        probs = [(score_ref[r, :, at] * inverse[r]).astype(jnp.bfloat16) for r in range(rows)]
        mixed = mixed + lax.dot_general(
            jnp.concatenate(probs),
            pool_ref[:KVR, at],
            (((1,), (1,)), ((), ())),
            preferred_element_type=jnp.float32,
        )
    out_ref[...] = mixed.reshape(out_ref.shape).astype(out_ref.dtype)


def attend_cached(queries, query_ids, latent_pool, key_owner):
    rows, heads, latent = queries.shape
    keys = latent_pool.shape[0]
    return pl.pallas_call(
        cached_kernel,
        out_shape=jax.ShapeDtypeStruct((rows, heads, KVR), jnp.bfloat16),
        in_specs=[pl.BlockSpec(memory_space=pltpu.SMEM)]
        + [pl.BlockSpec(memory_space=pltpu.VMEM)] * 3,
        out_specs=pl.BlockSpec(memory_space=pltpu.VMEM),
        scratch_shapes=[pltpu.VMEM((rows, heads, keys), jnp.float32)],
        compiler_params=pltpu.CompilerParams(vmem_limit_bytes=40 << 20),
        cost_estimate=pl.CostEstimate(
            flops=2 * rows * heads * keys * (latent + KVR),
            bytes_accessed=2 * keys * latent,
            transcendentals=rows * heads * keys,
        ),
    )(query_ids, key_owner.reshape(1, keys), jnp.swapaxes(queries, 1, 2), latent_pool.T)


def attend_new(queries, query_ids, pages, source_of, length_of):
    bf16, f32 = jnp.bfloat16, jnp.float32
    slots, new_len, latent_width = pages.shape
    token_iota = jnp.arange(new_len, dtype=jnp.int32)
    matching = query_ids[:, None] - RES == source_of[None, :]
    new_keys = jnp.dot(
        matching.astype(bf16), pages.reshape(slots, -1), preferred_element_type=f32
    ).astype(bf16)
    new_keys = new_keys.reshape(-1, new_len, latent_width)
    row_length = jnp.sum(jnp.where(matching, length_of[None, :], 0), axis=1)
    valid = (token_iota[None, :] < row_length[:, None])[:, None, :]
    scores = jnp.einsum("rhl,rnl->rhn", queries, new_keys, preferred_element_type=f32)
    scores = jnp.where(valid, scores * score_scale, -jnp.inf)
    weights = jnp.where(valid, jnp.exp(scores - jnp.max(scores, axis=-1, keepdims=True)), 0.0)
    probs = (weights / jnp.sum(weights, axis=-1, keepdims=True)).astype(bf16)
    return jnp.einsum("rhn,rnv->rhv", probs, new_keys[:, :, :KVR], preferred_element_type=f32)


def shards(
    rows_in,
    expert_ids,
    gate_values,
    w_gate,
    w_up,
    w_down,
    queries,
    query_ids,
    latent_pool,
    key_owner,
    sent_pages,
    sent_length,
    sent_rank,
):
    bf16, f32 = jnp.bfloat16, jnp.float32
    rows, width = rows_in.shape
    half = width // NC
    z, core = lax.axis_index("z"), lax.axis_index("c")
    place = lax.axis_index(("z", "x", "y", "c"))
    rank_count = NZ * NX * NY * NC
    plane = NX * NY
    block = plane * NC * rows
    new_len, latent_width = sent_pages.shape
    hid = w_gate.shape[1]

    def halves(value, axis):
        size = value.shape[axis] // NC
        mine = lax.dynamic_slice_in_dim(value, core * size, size, axis)
        theirs = lax.dynamic_slice_in_dim(value, (1 - core) * size, size, axis)
        return mine, shift(theirs, "c", 1)

    def in_order(mine, other, axis):
        return jnp.where(
            core == 0,
            jnp.concatenate([mine, other], axis=axis),
            jnp.concatenate([other, mine], axis=axis),
        )

    mine, other = halves(rows_in, 1)
    expert_iota = jnp.arange(EXPERTS, dtype=jnp.int32)
    matches = expert_ids[:, :, None] == expert_iota[None, None]
    weight = jnp.sum(jnp.where(matches, gate_values.astype(f32)[:, :, None], 0.0), axis=1)
    weight = weight.astype(bf16)
    expert_iota = expert_iota[None]
    chip_rows = in_order(mine, other, 0)
    chip_weight = in_order(weight, shift(weight, "c", 1), 0)

    wide = latent_width // 2
    piece = jnp.concatenate(
        [sent_pages[:, n * wide : (n + 1) * wide].reshape(plane, -1, wide) for n in range(2)],
        axis=1,
    )
    facts = jnp.concatenate([sent_length, sent_rank, place[None] + 1]).astype(bf16)
    facts = jnp.broadcast_to(facts[None, None], (plane, NC * rows, 3))
    spread = jnp.concatenate(
        [
            jnp.broadcast_to(chip_rows[None], (plane,) + chip_rows.shape),
            piece,
            jnp.broadcast_to(chip_weight[None], (plane,) + chip_weight.shape),
            facts,
        ],
        axis=2,
    )
    used = spread.shape[2]
    spread = jnp.pad(spread, ((0, 0), (0, 0), (0, -used % 128))).reshape(block, -1)
    at_weight = half + wide
    at_facts = at_weight + EXPERTS - half

    spread, ids = tie(spread, query_ids)
    own = lax.all_to_all(spread, ("x", "y"), split_axis=0, concat_axis=0, tiled=True)

    mixed = attend_cached(queries, ids, latent_pool, key_owner)
    own, mixed, w_gate, w_up, w_down = tie(own, mixed, w_gate, w_up, w_down)

    gate_mine, gate_other = halves(w_gate, 0)
    up_mine, up_other = halves(w_up, 0)
    down_mine, down_other = halves(w_down, 1)
    expert = z * (EXPERTS // NZ) + lax.axis_index("x") // (NX * NZ // EXPERTS)

    def enter(*data):
        data = jnp.concatenate(data)
        proj = jnp.dot(data[:, :half], w_in, preferred_element_type=f32)
        scale = jnp.sum(
            jnp.where(
                expert_iota == expert, data[:, at_weight : at_weight + EXPERTS].astype(f32), 0.0
            ),
            axis=1,
            keepdims=True,
        )
        return proj, scale, shift(proj, "c", 1)

    def leave(proj, scale, came):
        swapped = jnp.concatenate(
            [came[:, hid : 2 * hid], came[:, :hid], came[:, 3 * hid :], came[:, 2 * hid : 3 * hid]],
            axis=1,
        )
        proj = proj + swapped
        hidden = (jax.nn.silu(proj[:, : 2 * hid]) * proj[:, 2 * hid :]).astype(bf16)
        return jnp.dot(hidden, w_out, preferred_element_type=f32) * scale

    def send(pair):
        return shift(pair[0], "z", 1), shift(pair[1], "z", -1)

    def after(pair, *others):
        tied = tie(*pair, *others)
        return tied[:2], *tied[2:]

    rest = block // 2
    top, low = own[:rest], own[rest:]
    lead, back = (top, low), (low, top)
    lead1 = send(lead)
    back, gate_mine, up_mine, down_mine = after(back, gate_mine, up_mine, down_mine)
    back1 = send(back)
    w_in = jnp.concatenate([gate_mine, gate_other, up_mine, up_other], axis=1)
    w_out = jnp.concatenate([down_mine, down_other], axis=0)
    lead1, w_in, w_out, *_ = after(lead1, w_in, w_out, *back)
    lead2 = send(lead1)
    proj0, scale0, came0 = enter(top, low)
    back1, proj0, scale0, *_ = after(back1, proj0, scale0, *lead1)
    back2 = send(back1)
    proj1, scale1, came1 = enter(*lead1, *back1)
    lead2, proj1, scale1, came0, *_ = after(lead2, proj1, scale1, came0, *back1)
    lead3 = send(lead2)
    part0 = leave(proj0, scale0, came0)
    back2, came1, part0, *_ = after(back2, came1, part0, *lead2)
    back3 = send(back2)
    proj2, scale2, came2 = enter(*lead2, *back2)
    lead3, proj2, scale2, came1, *_ = after(lead3, proj2, scale2, came1, *back2)
    lead4 = send(lead3)
    part1 = leave(proj1, scale1, came1)
    back3, came2, part1, *_ = after(back3, came2, part1, *lead3)
    proj3, scale3, came3 = enter(*lead3, *back3)
    part2 = leave(proj2, scale2, came2)
    lead4, proj3, scale3, part2 = after(lead4, proj3, scale3, part2)
    proj4, scale4, came4 = enter(*lead4)
    proj4, came3 = tie(proj4, came3)
    part3 = leave(proj3, scale3, came3)
    part4 = leave(proj4, scale4, came4)

    def of(part, n):
        return part[n * rest : (n + 1) * rest]

    def add(got, part, first, second):
        pair = zip(got, (of(part, first), of(part, second)))
        return tie(*((g.astype(f32) + p).astype(bf16) for g, p in pair))

    lead = tie(of(part4, 0).astype(bf16), of(part4, 1).astype(bf16))
    back = tie(of(part3, 1).astype(bf16), of(part3, 0).astype(bf16))
    parts = {3: part3, 2: part2, 1: part1}
    pieces = (own, *lead1, *back1, *lead2, *back2, *lead3, *back3, *lead4)
    pieces = jnp.concatenate([p[:, half:] for p in pieces])
    lead_got, back_got = send(lead), send(back)
    for k in (3, 2, 1):
        lead_got, *_ = after(lead_got, *back)
        if k == 1:
            lead_got, bound = after(lead_got, bound)
        lead = add(lead_got, parts[k], 3, 2)
        lead_got = send(lead)
        if k > 1:
            back_got, *_ = after(back_got, *lead)
            back = add(back_got, parts[k - 1], 1, 0)
            back_got = send(back)
        if k == 3:
            pieces, *_ = tie(pieces, *lead)
            pieces = pieces.reshape(NZ * plane, NC * rows, -1)
            ranks = pieces[:, 0, at_facts + 1].astype(jnp.int32)
            source = jnp.arange(NZ * plane, dtype=jnp.int32)
            same = (ranks[:, None] == ranks[None, :]) & (source[None, :] < source[:, None])
            turn = jnp.sum(same.astype(jnp.int32), axis=1)
            here = z * (plane * NC) + jnp.arange(plane * NC, dtype=jnp.int32)
            slot = jnp.arange(NEWMAX, dtype=jnp.int32)
            selected = (ranks == here[:, None, None]) & (turn == slot[None, :, None])
            selected = selected.reshape(plane, NC * NEWMAX, NZ * plane).astype(bf16)
            bound = jnp.einsum("pks,sij->pikj", selected, pieces, preferred_element_type=f32)
            bound = bound.astype(bf16).reshape(plane, NC * rows, NC, -1)
            mine = lax.dynamic_index_in_dim(bound, core, 2, keepdims=False)
            theirs = lax.dynamic_index_in_dim(bound, 1 - core, 2, keepdims=False)
            theirs = shift(theirs, "c", 1)
        if k == 2:
            bound = jnp.concatenate([mine, theirs], axis=2).reshape(block, -1)
            bound, *_ = tie(bound, *lead)
            bound = lax.ppermute(bound, "g", [(0, 1)])
    total = [
        of(part0, 0) + lead_got[0].astype(f32) + back_got[1].astype(f32),
        of(part0, 1) + back_got[0].astype(f32) + lead_got[1].astype(f32),
    ]
    total = jnp.concatenate(total).astype(bf16)
    total = jnp.concatenate([total, bound], axis=1)
    total = lax.all_to_all(total, ("x", "y"), split_axis=0, concat_axis=0, tiled=True)
    got = total[:, half:]
    total = jnp.sum(total[:, :half].reshape(plane, NC * rows, half).astype(f32), axis=0)
    total = total.astype(bf16)
    mine = lax.dynamic_slice_in_dim(total, core * rows, rows, 0)
    other = shift(lax.dynamic_slice_in_dim(total, (1 - core) * rows, rows, 0), "c", 1)
    expert_out = in_order(mine, other, 1)

    got = got.reshape(plane, 2, rows, NC * NEWMAX, -1)
    pages = jnp.concatenate([got[:, 0, :, :, :wide], got[:, 1, :, :, :wide]], axis=-1)
    pages = jnp.transpose(pages, (2, 0, 1, 3)).reshape(NC * NEWMAX, new_len, latent_width)
    facts = got[0, 0, 0, :, at_facts : at_facts + 3].astype(jnp.int32)
    mixed_new = attend_new(queries, query_ids, pages, facts[:, 2] - 1, facts[:, 0])
    attention = jnp.where(query_ids[:, None, None] >= RES, mixed_new.astype(bf16), mixed)
    return (expert_out, attention)


def solution(mesh):
    fine = Mesh(mesh.devices.reshape(2, NZ, NX, NY, NC), ALL)
    placed = (
        P(ALL, None),
        P(ALL, None),
        P(ALL, None),
        P(None, EP),
        P(None, EP),
        P(EP, None),
        P(ALL, None, None),
        P(ALL),
        P(ALL, None),
        P(ALL),
        P(ALL, None),
        P(ALL),
        P(ALL),
    )
    return jax.shard_map(
        shards,
        mesh=fine,
        in_specs=placed,
        out_specs=(P(ALL, None), P(ALL, None, None)),
        check_vma=False,
    )
```

```python
import jax
import jax.numpy as jnp
from jax import lax
from jax.experimental import pallas as pl
from jax.experimental.pallas import tpu as pltpu
from jax.sharding import Mesh, PartitionSpec as P

EXPERTS = 16
KVR = 512
RES = 4
NEWMAX = 2
NZ, NX, NY, NC = 8, 4, 2, 2
EP = ("z", "x", "y", "c")
ALL = ("g",) + EP

score_scale = 192.0 ** (-0.5)


def shift(value, axis, by):
    length = lax.axis_size(axis)
    return lax.ppermute(value, axis, [(i, (i + by) % length) for i in range(length)])


def tie(*values):
    return lax.optimization_barrier(values)


def cached_kernel(ids_ref, owner_ref, q_ref, pool_ref, out_ref, score_ref):
    rows, _, heads = q_ref.shape
    keys = pool_ref.shape[1]
    step, lanes = 512, 128
    columns = [slice(n * lanes, (n + 1) * lanes) for n in range(step // lanes)]
    blocks = [slice(n, n + step) for n in range(0, keys, step)]
    queries = jnp.concatenate([q_ref[r] for r in range(rows)], axis=1).T
    tops = [jnp.full((heads, lanes), -jnp.inf, jnp.float32) for _ in range(rows)]
    for at in blocks:
        scores = jnp.dot(queries, pool_ref[:, at], preferred_element_type=jnp.float32)
        for r in range(rows):
            part = scores[r * heads : (r + 1) * heads] * score_scale
            part = jnp.where(owner_ref[:, at] == ids_ref[r], part, -jnp.inf)
            score_ref[r, :, at] = part
            for column in columns:
                tops[r] = jnp.maximum(tops[r], part[:, column])
    inverse = []
    for r in range(rows):
        top = jnp.maximum(jnp.max(tops[r], axis=1, keepdims=True), -3e38)
        total = jnp.zeros((heads, lanes), jnp.float32)
        for at in blocks:
            part = jnp.exp(score_ref[r, :, at] - top)
            score_ref[r, :, at] = part
            for column in columns:
                total = total + part[:, column]
        inverse.append(1.0 / jnp.maximum(jnp.sum(total, axis=1, keepdims=True), 1e-30))
    mixed = jnp.zeros((rows * heads, KVR), jnp.float32)
    for at in blocks:
        probs = [(score_ref[r, :, at] * inverse[r]).astype(jnp.bfloat16) for r in range(rows)]
        mixed = mixed + lax.dot_general(
            jnp.concatenate(probs),
            pool_ref[:KVR, at],
            (((1,), (1,)), ((), ())),
            preferred_element_type=jnp.float32,
        )
    out_ref[...] = mixed.reshape(out_ref.shape).astype(out_ref.dtype)


def attend_cached(queries, query_ids, latent_pool, key_owner):
    rows, heads, latent = queries.shape
    keys = latent_pool.shape[0]
    return pl.pallas_call(
        cached_kernel,
        out_shape=jax.ShapeDtypeStruct((rows, heads, KVR), jnp.bfloat16),
        in_specs=[pl.BlockSpec(memory_space=pltpu.SMEM)]
        + [pl.BlockSpec(memory_space=pltpu.VMEM)] * 3,
        out_specs=pl.BlockSpec(memory_space=pltpu.VMEM),
        scratch_shapes=[pltpu.VMEM((rows, heads, keys), jnp.float32)],
        compiler_params=pltpu.CompilerParams(vmem_limit_bytes=20 << 20),
        cost_estimate=pl.CostEstimate(
            flops=2 * rows * heads * keys * (latent + KVR),
            bytes_accessed=2 * keys * latent,
            transcendentals=rows * heads * keys,
        ),
    )(query_ids, key_owner.reshape(1, keys), jnp.swapaxes(queries, 1, 2), latent_pool.T)


def choose_kernel(at_ref, rank_lane, group, pieces_ref, mine_ref, their_ref):
    bf16, f32, i32 = jnp.bfloat16, jnp.float32, jnp.int32
    pieces = pieces_ref[...]
    count, lanes = pieces.shape
    sources = count // group
    rows = mine_ref.shape[0]

    def iota(shape, axis):
        return lax.broadcasted_iota(i32, shape, axis)

    pick = iota((sources, count), 1) == iota((sources, count), 0) * group
    facts = jnp.dot(pick.astype(bf16), pieces, preferred_element_type=f32)
    lane = (iota((8, lanes), 1) == rank_lane).astype(bf16)
    along = lax.dot_general(
        lane, facts.astype(bf16), (((1,), (1,)), ((), ())), preferred_element_type=f32
    )
    down = facts[:, rank_lane : rank_lane + 1]
    earlier = iota((sources, sources), 0) < iota((sources, sources), 1)
    turn = jnp.where((down == along[:1]) & earlier, 1.0, 0.0)
    turn = jnp.sum(turn, axis=0, keepdims=True)
    repeat = (iota((sources, count), 1) // group == iota((sources, count), 0)).astype(bf16)
    along = jnp.dot(along.astype(bf16), repeat, preferred_element_type=f32)[:1].astype(i32)
    turn = jnp.broadcast_to(turn, (8, sources)).astype(bf16)
    turn = jnp.dot(turn, repeat, preferred_element_type=f32)[:1].astype(i32)
    row, column = iota((rows, count), 0), iota((rows, count), 1)
    aligned = row % group == column % group
    for side, target in ((at_ref[1], mine_ref), (1 - at_ref[1], their_ref)):
        here = at_ref[0] + row // group * NC + side
        for slot in range(NEWMAX):
            chosen = aligned & (along == here) & (turn == slot)
            target[:, slot * lanes : (slot + 1) * lanes] = jnp.dot(
                chosen.astype(bf16), pieces, preferred_element_type=f32
            ).astype(bf16)


def choose(pieces, first, core, rank_lane, group, rows):
    shape = jax.ShapeDtypeStruct((rows, NEWMAX * pieces.shape[1]), jnp.bfloat16)
    vmem = pl.BlockSpec(memory_space=pltpu.VMEM)

    def kernel(at_ref, pieces_ref, mine_ref, their_ref):
        choose_kernel(at_ref, rank_lane, group, pieces_ref, mine_ref, their_ref)

    return pl.pallas_call(
        kernel,
        out_shape=(shape, shape),
        in_specs=[pl.BlockSpec(memory_space=pltpu.SMEM), vmem],
        out_specs=(vmem, vmem),
        compiler_params=pltpu.CompilerParams(vmem_limit_bytes=8 << 20),
        cost_estimate=pl.CostEstimate(
            flops=8 * pieces.size * rows, bytes_accessed=4 * pieces.size, transcendentals=0
        ),
    )(jnp.stack([first, core]), pieces)


def attend_new(queries, query_ids, pages, source_of, length_of):
    bf16, f32 = jnp.bfloat16, jnp.float32
    slots, new_len, latent_width = pages.shape
    token_iota = jnp.arange(new_len, dtype=jnp.int32)
    matching = query_ids[:, None] - RES == source_of[None, :]
    new_keys = jnp.dot(
        matching.astype(bf16), pages.reshape(slots, -1), preferred_element_type=f32
    ).astype(bf16)
    new_keys = new_keys.reshape(-1, new_len, latent_width)
    row_length = jnp.sum(jnp.where(matching, length_of[None, :], 0), axis=1)
    valid = (token_iota[None, :] < row_length[:, None])[:, None, :]
    scores = jnp.einsum("rhl,rnl->rhn", queries, new_keys, preferred_element_type=f32)
    scores = jnp.where(valid, scores * score_scale, -jnp.inf)
    weights = jnp.where(valid, jnp.exp(scores - jnp.max(scores, axis=-1, keepdims=True)), 0.0)
    probs = (weights / jnp.sum(weights, axis=-1, keepdims=True)).astype(bf16)
    return jnp.einsum("rhn,rnv->rhv", probs, new_keys[:, :, :KVR], preferred_element_type=f32)


def shards(
    rows_in,
    expert_ids,
    gate_values,
    w_gate,
    w_up,
    w_down,
    queries,
    query_ids,
    latent_pool,
    key_owner,
    sent_pages,
    sent_length,
    sent_rank,
):
    bf16, f32 = jnp.bfloat16, jnp.float32
    rows, width = rows_in.shape
    half = width // NC
    z, core = lax.axis_index("z"), lax.axis_index("c")
    place = lax.axis_index(("z", "x", "y", "c"))
    rank_count = NZ * NX * NY * NC
    plane = NX * NY
    block = plane * NC * rows
    new_len, latent_width = sent_pages.shape
    hid = w_gate.shape[1]

    def halves(value, axis):
        size = value.shape[axis] // NC
        mine = lax.dynamic_slice_in_dim(value, core * size, size, axis)
        theirs = lax.dynamic_slice_in_dim(value, (1 - core) * size, size, axis)
        return mine, shift(theirs, "c", 1)

    def in_order(mine, other, axis):
        return jnp.where(
            core == 0,
            jnp.concatenate([mine, other], axis=axis),
            jnp.concatenate([other, mine], axis=axis),
        )

    mine, other = halves(rows_in, 1)
    expert_iota = jnp.arange(EXPERTS, dtype=jnp.int32)
    matches = expert_ids[:, :, None] == expert_iota[None, None]
    weight = jnp.sum(jnp.where(matches, gate_values.astype(f32)[:, :, None], 0.0), axis=1)
    weight = weight.astype(bf16)
    expert_iota = expert_iota[None]
    chip_rows = in_order(mine, other, 0)
    chip_weight = in_order(weight, shift(weight, "c", 1), 0)

    wide = latent_width // 2
    piece = jnp.concatenate(
        [sent_pages[:, n * wide : (n + 1) * wide].reshape(plane, -1, wide) for n in range(2)],
        axis=1,
    )
    facts = jnp.concatenate([sent_length, sent_rank, place[None] + 1]).astype(bf16)
    facts = jnp.broadcast_to(facts[None, None], (plane, NC * rows, 3))
    spread = jnp.concatenate(
        [
            jnp.broadcast_to(chip_rows[None], (plane,) + chip_rows.shape),
            piece,
            jnp.broadcast_to(chip_weight[None], (plane,) + chip_weight.shape),
            facts,
        ],
        axis=2,
    )
    used = spread.shape[2]
    spread = jnp.pad(spread, ((0, 0), (0, 0), (0, -used % 128))).reshape(block, -1)
    at_weight = half + wide
    at_facts = at_weight + EXPERTS - half

    spread, ids = tie(spread, query_ids)
    own = lax.all_to_all(spread, ("x", "y"), split_axis=0, concat_axis=0, tiled=True)

    mixed = attend_cached(queries, ids, latent_pool, key_owner)
    own, mixed, w_gate, w_up, w_down = tie(own, mixed, w_gate, w_up, w_down)

    gate_mine, gate_other = halves(w_gate, 0)
    up_mine, up_other = halves(w_up, 0)
    down_mine, down_other = halves(w_down, 1)
    expert = z * (EXPERTS // NZ) + lax.axis_index("x") // (NX * NZ // EXPERTS)

    def enter(*data):
        data = jnp.concatenate(data)
        proj = jnp.dot(data[:, :half], w_in, preferred_element_type=f32)
        scale = jnp.sum(
            jnp.where(
                expert_iota == expert, data[:, at_weight : at_weight + EXPERTS].astype(f32), 0.0
            ),
            axis=1,
            keepdims=True,
        )
        return proj, scale, shift(proj, "c", 1)

    def leave(proj, scale, came):
        swapped = jnp.concatenate(
            [came[:, hid : 2 * hid], came[:, :hid], came[:, 3 * hid :], came[:, 2 * hid : 3 * hid]],
            axis=1,
        )
        proj = proj + swapped
        hidden = (jax.nn.silu(proj[:, : 2 * hid]) * proj[:, 2 * hid :]).astype(bf16)
        return jnp.dot(hidden, w_out, preferred_element_type=f32) * scale

    def send(pair):
        return shift(pair[0], "z", 1), shift(pair[1], "z", -1)

    def after(pair, *others):
        tied = tie(*pair, *others)
        return tied[:2], *tied[2:]

    rest = block // 2
    top, low = own[:rest], own[rest:]
    lead, back = (top, low), (low, top)
    lead1 = send(lead)
    back, gate_mine, up_mine, down_mine = after(back, gate_mine, up_mine, down_mine)
    back1 = send(back)
    w_in = jnp.concatenate([gate_mine, gate_other, up_mine, up_other], axis=1)
    w_out = jnp.concatenate([down_mine, down_other], axis=0)
    lead1, w_in, w_out, *_ = after(lead1, w_in, w_out, *back)
    lead2 = send(lead1)
    back1, *_ = after(back1, *lead1)
    back2 = send(back1)
    proj0, scale0, came0 = enter(top, low, *lead1, *back1)
    lead2, proj0, scale0, *_ = after(lead2, proj0, scale0, *back1)
    lead3 = send(lead2)
    back2, came0, *_ = after(back2, came0, *lead2)
    back3 = send(back2)
    proj2, scale2, came2 = enter(*lead2, *back2)
    part0 = leave(proj0, scale0, came0)
    lead3, proj2, scale2, part0, *_ = after(lead3, proj2, scale2, part0, *back2)
    lead4 = send(lead3)
    back3, came2, *_ = after(back3, came2, *lead3)
    proj3, scale3, came3 = enter(*lead3, *back3)
    part2 = leave(proj2, scale2, came2)
    lead4, proj3, scale3, part2 = after(lead4, proj3, scale3, part2)
    proj4, scale4, came4 = enter(*lead4)
    proj4, came3 = tie(proj4, came3)
    part3 = leave(proj3, scale3, came3)
    part4 = leave(proj4, scale4, came4)

    def of(part, n):
        return part[n * rest : (n + 1) * rest]

    def add(got, mine, first, second):
        part, offset = mine
        pair = zip(got, (of(part, offset + first), of(part, offset + second)))
        return tie(*((g.astype(f32) + p).astype(bf16) for g, p in pair))

    lead = tie(of(part4, 0).astype(bf16), of(part4, 1).astype(bf16))
    back = tie(of(part3, 1).astype(bf16), of(part3, 0).astype(bf16))
    parts = {3: (part3, 0), 2: (part2, 0), 1: (part0, 2)}
    pieces = (own, *lead1, *back1, *lead2, *back2, *lead3, *back3, *lead4)
    pieces = jnp.concatenate([p[:, half:] for p in pieces])
    lead_got, back_got = send(lead), send(back)
    for k in (3, 2, 1):
        lead_got, *_ = after(lead_got, *back)
        if k == 1:
            lead_got, bound = after(lead_got, bound)
        lead = add(lead_got, parts[k], 3, 2)
        lead_got = send(lead)
        if k > 1:
            back_got, *_ = after(back_got, *lead)
            back = add(back_got, parts[k - 1], 1, 0)
            back_got = send(back)
        if k == 3:
            pieces, *_ = tie(pieces, *lead)
            mine, theirs = choose(
                pieces, z * (plane * NC), core, at_facts + 1, NC * rows, block
            )
            theirs = shift(theirs, "c", 1)
        if k == 2:
            bound = jnp.concatenate([mine, theirs], axis=1)
            bound, *_ = tie(bound, *lead)
            bound = lax.ppermute(bound, "g", [(0, 1)])
    total = [
        of(part0, 0) + lead_got[0].astype(f32) + back_got[1].astype(f32),
        of(part0, 1) + back_got[0].astype(f32) + lead_got[1].astype(f32),
    ]
    total = jnp.concatenate(total).astype(bf16)
    total = jnp.concatenate([total, bound], axis=1)
    total = lax.all_to_all(total, ("x", "y"), split_axis=0, concat_axis=0, tiled=True)
    got = total[:, half:]
    total = jnp.sum(total[:, :half].reshape(plane, NC * rows, half).astype(f32), axis=0)
    total = total.astype(bf16)
    mine = lax.dynamic_slice_in_dim(total, core * rows, rows, 0)
    other = shift(lax.dynamic_slice_in_dim(total, (1 - core) * rows, rows, 0), "c", 1)
    expert_out = in_order(mine, other, 1)

    got = got.reshape(plane, 2, rows, NC * NEWMAX, -1)
    pages = jnp.concatenate([got[:, 0, :, :, :wide], got[:, 1, :, :, :wide]], axis=-1)
    pages = jnp.transpose(pages, (2, 0, 1, 3)).reshape(NC * NEWMAX, new_len, latent_width)
    facts = got[0, 0, 0, :, at_facts : at_facts + 3].astype(jnp.int32)
    mixed_new = attend_new(queries, query_ids, pages, facts[:, 2] - 1, facts[:, 0])
    attention = jnp.where(query_ids[:, None, None] >= RES, mixed_new.astype(bf16), mixed)
    return (expert_out, attention)


def solution(mesh):
    fine = Mesh(mesh.devices.reshape(2, NZ, NX, NY, NC), ALL)
    placed = (
        P(ALL, None),
        P(ALL, None),
        P(ALL, None),
        P(None, EP),
        P(None, EP),
        P(EP, None),
        P(ALL, None, None),
        P(ALL),
        P(ALL, None),
        P(ALL),
        P(ALL, None),
        P(ALL),
        P(ALL),
    )
    return jax.shard_map(
        shards,
        mesh=fine,
        in_specs=placed,
        out_specs=(P(ALL, None), P(ALL, None, None)),
        check_vma=False,
    )
```

```python
import jax
import jax.numpy as jnp
from jax import lax
from jax.experimental import pallas as pl
from jax.experimental.pallas import tpu as pltpu
from jax.sharding import Mesh, PartitionSpec as P

EXPERTS = 16
KVR = 512
RES = 4
NEWMAX = 2
NZ, NX, NY, NC = 8, 4, 2, 2
EP = ("z", "x", "y", "c")
ALL = ("g",) + EP

score_scale = 192.0 ** (-0.5)


def shift(value, axis, by):
    length = lax.axis_size(axis)
    return lax.ppermute(value, axis, [(i, (i + by) % length) for i in range(length)])


def tie(*values):
    return lax.optimization_barrier(values)


def cached_kernel(ids_ref, owner_ref, q_ref, pool_ref, out_ref, score_ref):
    rows, _, heads = q_ref.shape
    keys = pool_ref.shape[1]
    step, lanes = 512, 128
    columns = [slice(n * lanes, (n + 1) * lanes) for n in range(step // lanes)]
    blocks = [slice(n, n + step) for n in range(0, keys, step)]
    queries = jnp.concatenate([q_ref[r] for r in range(rows)], axis=1).T
    tops = [jnp.full((heads, lanes), -jnp.inf, jnp.float32) for _ in range(rows)]
    for at in blocks:
        scores = jnp.dot(queries, pool_ref[:, at], preferred_element_type=jnp.float32)
        for r in range(rows):
            part = scores[r * heads : (r + 1) * heads] * score_scale
            part = jnp.where(owner_ref[:, at] == ids_ref[r], part, -jnp.inf)
            score_ref[r, :, at] = part
            for column in columns:
                tops[r] = jnp.maximum(tops[r], part[:, column])
    inverse = []
    for r in range(rows):
        top = jnp.maximum(jnp.max(tops[r], axis=1, keepdims=True), -3e38)
        total = jnp.zeros((heads, lanes), jnp.float32)
        for at in blocks:
            part = jnp.exp(score_ref[r, :, at] - top)
            score_ref[r, :, at] = part
            for column in columns:
                total = total + part[:, column]
        inverse.append(1.0 / jnp.maximum(jnp.sum(total, axis=1, keepdims=True), 1e-30))
    mixed = jnp.zeros((rows * heads, KVR), jnp.float32)
    for at in blocks:
        probs = [(score_ref[r, :, at] * inverse[r]).astype(jnp.bfloat16) for r in range(rows)]
        mixed = mixed + lax.dot_general(
            jnp.concatenate(probs),
            pool_ref[:KVR, at],
            (((1,), (1,)), ((), ())),
            preferred_element_type=jnp.float32,
        )
    out_ref[...] = mixed.reshape(out_ref.shape).astype(out_ref.dtype)


def attend_cached(queries, query_ids, latent_pool, key_owner):
    rows, heads, latent = queries.shape
    keys = latent_pool.shape[0]
    return pl.pallas_call(
        cached_kernel,
        out_shape=jax.ShapeDtypeStruct((rows, heads, KVR), jnp.bfloat16),
        in_specs=[pl.BlockSpec(memory_space=pltpu.SMEM)]
        + [pl.BlockSpec(memory_space=pltpu.VMEM)] * 3,
        out_specs=pl.BlockSpec(memory_space=pltpu.VMEM),
        scratch_shapes=[pltpu.VMEM((rows, heads, keys), jnp.float32)],
        compiler_params=pltpu.CompilerParams(vmem_limit_bytes=20 << 20),
        cost_estimate=pl.CostEstimate(
            flops=2 * rows * heads * keys * (latent + KVR),
            bytes_accessed=2 * keys * latent,
            transcendentals=rows * heads * keys,
        ),
    )(query_ids, key_owner.reshape(1, keys), jnp.swapaxes(queries, 1, 2), latent_pool.T)


def choose_kernel(at_ref, rank_lane, group, pieces_ref, mine_ref, their_ref):
    bf16, f32, i32 = jnp.bfloat16, jnp.float32, jnp.int32
    pieces = pieces_ref[...]
    count, lanes = pieces.shape
    sources = count // group
    rows = mine_ref.shape[0]

    def iota(shape, axis):
        return lax.broadcasted_iota(i32, shape, axis)

    pick = iota((sources, count), 1) == iota((sources, count), 0) * group
    facts = jnp.dot(pick.astype(bf16), pieces, preferred_element_type=f32)
    lane = (iota((8, lanes), 1) == rank_lane).astype(bf16)
    along = lax.dot_general(
        lane, facts.astype(bf16), (((1,), (1,)), ((), ())), preferred_element_type=f32
    )
    down = facts[:, rank_lane : rank_lane + 1]
    earlier = iota((sources, sources), 0) < iota((sources, sources), 1)
    turn = jnp.where((down == along[:1]) & earlier, 1.0, 0.0)
    turn = jnp.sum(turn, axis=0, keepdims=True)
    repeat = (iota((sources, count), 1) // group == iota((sources, count), 0)).astype(bf16)
    along = jnp.dot(along.astype(bf16), repeat, preferred_element_type=f32)[:1].astype(i32)
    turn = jnp.broadcast_to(turn, (8, sources)).astype(bf16)
    turn = jnp.dot(turn, repeat, preferred_element_type=f32)[:1].astype(i32)
    row, column = iota((rows, count), 0), iota((rows, count), 1)
    aligned = row % group == column % group
    for side, target in ((at_ref[1], mine_ref), (1 - at_ref[1], their_ref)):
        here = at_ref[0] + row // group * NC + side
        for slot in range(NEWMAX):
            chosen = aligned & (along == here) & (turn == slot)
            target[:, slot * lanes : (slot + 1) * lanes] = jnp.dot(
                chosen.astype(bf16), pieces, preferred_element_type=f32
            ).astype(bf16)


def choose(pieces, first, core, rank_lane, group, rows):
    shape = jax.ShapeDtypeStruct((rows, NEWMAX * pieces.shape[1]), jnp.bfloat16)
    vmem = pl.BlockSpec(memory_space=pltpu.VMEM)

    def kernel(at_ref, pieces_ref, mine_ref, their_ref):
        choose_kernel(at_ref, rank_lane, group, pieces_ref, mine_ref, their_ref)

    return pl.pallas_call(
        kernel,
        out_shape=(shape, shape),
        in_specs=[pl.BlockSpec(memory_space=pltpu.SMEM), vmem],
        out_specs=(vmem, vmem),
        compiler_params=pltpu.CompilerParams(vmem_limit_bytes=8 << 20),
        cost_estimate=pl.CostEstimate(
            flops=8 * pieces.size * rows, bytes_accessed=4 * pieces.size, transcendentals=0
        ),
    )(jnp.stack([first, core]), pieces)


def attend_new(queries, query_ids, pages, source_of, length_of):
    bf16, f32 = jnp.bfloat16, jnp.float32
    slots, new_len, latent_width = pages.shape
    token_iota = jnp.arange(new_len, dtype=jnp.int32)
    matching = query_ids[:, None] - RES == source_of[None, :]
    new_keys = jnp.dot(
        matching.astype(bf16), pages.reshape(slots, -1), preferred_element_type=f32
    ).astype(bf16)
    new_keys = new_keys.reshape(-1, new_len, latent_width)
    row_length = jnp.sum(jnp.where(matching, length_of[None, :], 0), axis=1)
    valid = (token_iota[None, :] < row_length[:, None])[:, None, :]
    scores = jnp.einsum("rhl,rnl->rhn", queries, new_keys, preferred_element_type=f32)
    scores = jnp.where(valid, scores * score_scale, -jnp.inf)
    weights = jnp.where(valid, jnp.exp(scores - jnp.max(scores, axis=-1, keepdims=True)), 0.0)
    probs = (weights / jnp.sum(weights, axis=-1, keepdims=True)).astype(bf16)
    return jnp.einsum("rhn,rnv->rhv", probs, new_keys[:, :, :KVR], preferred_element_type=f32)


def shards(
    rows_in,
    expert_ids,
    gate_values,
    w_gate,
    w_up,
    w_down,
    queries,
    query_ids,
    latent_pool,
    key_owner,
    sent_pages,
    sent_length,
    sent_rank,
):
    bf16, f32 = jnp.bfloat16, jnp.float32
    rows, width = rows_in.shape
    half = width // NC
    z, core = lax.axis_index("z"), lax.axis_index("c")
    place = lax.axis_index(("z", "x", "y", "c"))
    rank_count = NZ * NX * NY * NC
    plane = NX * NY
    block = plane * NC * rows
    new_len, latent_width = sent_pages.shape
    hid = w_gate.shape[1]

    def halves(value, axis):
        size = value.shape[axis] // NC
        mine = lax.dynamic_slice_in_dim(value, core * size, size, axis)
        theirs = lax.dynamic_slice_in_dim(value, (1 - core) * size, size, axis)
        return mine, shift(theirs, "c", 1)

    def in_order(mine, other, axis):
        return jnp.where(
            core == 0,
            jnp.concatenate([mine, other], axis=axis),
            jnp.concatenate([other, mine], axis=axis),
        )

    mine, other = halves(rows_in, 1)
    expert_iota = jnp.arange(EXPERTS, dtype=jnp.int32)
    matches = expert_ids[:, :, None] == expert_iota[None, None]
    weight = jnp.sum(jnp.where(matches, gate_values[:, :, None], 0), axis=1, dtype=bf16)
    expert_iota = expert_iota[None]
    chip_rows = in_order(mine, other, 0)
    chip_weight = in_order(weight, shift(weight, "c", 1), 0)

    wide = latent_width // 2
    piece = jnp.concatenate(
        [sent_pages[:, n * wide : (n + 1) * wide].reshape(plane, -1, wide) for n in range(2)],
        axis=1,
    )
    facts = jnp.concatenate([sent_length, sent_rank, place[None] + 1]).astype(bf16)
    facts = jnp.broadcast_to(facts[None, None], (plane, NC * rows, 3))
    spread = jnp.concatenate(
        [
            jnp.broadcast_to(chip_rows[None], (plane,) + chip_rows.shape),
            piece,
            jnp.broadcast_to(chip_weight[None], (plane,) + chip_weight.shape),
            facts,
        ],
        axis=2,
    )
    used = spread.shape[2]
    spread = jnp.pad(spread, ((0, 0), (0, 0), (0, -used % 128))).reshape(block, -1)
    at_weight = half + wide
    at_facts = at_weight + EXPERTS - half

    spread, ids = tie(spread, query_ids)
    own = lax.all_to_all(spread, ("x", "y"), split_axis=0, concat_axis=0, tiled=True)

    mixed = attend_cached(queries, ids, latent_pool, key_owner)
    own, mixed, w_gate, w_up, w_down = tie(own, mixed, w_gate, w_up, w_down)

    gate_mine, gate_other = halves(w_gate, 0)
    up_mine, up_other = halves(w_up, 0)
    down_mine, down_other = halves(w_down, 1)
    expert = z * (EXPERTS // NZ) + lax.axis_index("x") // (NX * NZ // EXPERTS)

    def enter(*data):
        data = jnp.concatenate(data)
        proj = jnp.dot(data[:, :half], w_in, preferred_element_type=f32)
        scale = jnp.sum(
            jnp.where(
                expert_iota == expert, data[:, at_weight : at_weight + EXPERTS].astype(f32), 0.0
            ),
            axis=1,
            keepdims=True,
        )
        return proj, scale, shift(proj, "c", 1)

    def leave(proj, scale, came):
        swapped = jnp.concatenate(
            [came[:, hid : 2 * hid], came[:, :hid], came[:, 3 * hid :], came[:, 2 * hid : 3 * hid]],
            axis=1,
        )
        proj = proj + swapped
        hidden = (jax.nn.silu(proj[:, : 2 * hid]) * proj[:, 2 * hid :]).astype(bf16)
        return jnp.dot(hidden, w_out, preferred_element_type=f32) * scale

    def send(pair):
        return shift(pair[0], "z", 1), shift(pair[1], "z", -1)

    def after(pair, *others):
        tied = tie(*pair, *others)
        return tied[:2], *tied[2:]

    rest = block // 2
    top, low = own[:rest], own[rest:]
    lead, back = (top, low), (low, top)
    lead1 = send(lead)
    back, gate_mine, up_mine, down_mine = after(back, gate_mine, up_mine, down_mine)
    back1 = send(back)
    w_in = jnp.concatenate([gate_mine, gate_other, up_mine, up_other], axis=1)
    w_out = jnp.concatenate([down_mine, down_other], axis=0)
    lead1, w_in, w_out, *_ = after(lead1, w_in, w_out, *back)
    lead2 = send(lead1)
    back1, *_ = after(back1, *lead1)
    back2 = send(back1)
    proj0, scale0, came0 = enter(top, low, *lead1, *back1)
    lead2, proj0, scale0, *_ = after(lead2, proj0, scale0, *back1)
    lead3 = send(lead2)
    back2, came0, *_ = after(back2, came0, *lead2)
    back3 = send(back2)
    proj2, scale2, came2 = enter(*lead2, *back2)
    part0 = leave(proj0, scale0, came0)
    lead3, proj2, scale2, part0, *_ = after(lead3, proj2, scale2, part0, *back2)
    lead4 = send(lead3)
    back3, came2, *_ = after(back3, came2, *lead3)
    proj3, scale3, came3 = enter(*lead3, *back3)
    part2 = leave(proj2, scale2, came2)
    lead4, proj3, scale3, part2 = after(lead4, proj3, scale3, part2)
    proj4, scale4, came4 = enter(*lead4)
    proj4, came3 = tie(proj4, came3)
    part3 = leave(proj3, scale3, came3)
    part4 = leave(proj4, scale4, came4)

    def of(part, n):
        return part[n * rest : (n + 1) * rest]

    def add(got, mine, first, second):
        part, offset = mine
        pair = zip(got, (of(part, offset + first), of(part, offset + second)))
        return tie(*((g.astype(f32) + p).astype(bf16) for g, p in pair))

    lead = tie(of(part4, 0).astype(bf16), of(part4, 1).astype(bf16))
    back = tie(of(part3, 1).astype(bf16), of(part3, 0).astype(bf16))
    parts = {3: (part3, 0), 2: (part2, 0), 1: (part0, 2)}
    pieces = (own, *lead1, *back1, *lead2, *back2, *lead3, *back3, *lead4)
    pieces = jnp.concatenate([p[:, half:] for p in pieces])
    lead_got, back_got = send(lead), send(back)
    for k in (3, 2, 1):
        lead_got, *_ = after(lead_got, *back)
        if k == 1:
            lead_got, bound = after(lead_got, bound)
        lead = add(lead_got, parts[k], 3, 2)
        lead_got = send(lead)
        if k > 1:
            back_got, *_ = after(back_got, *lead)
            back = add(back_got, parts[k - 1], 1, 0)
            back_got = send(back)
        if k == 3:
            pieces, *_ = tie(pieces, *lead)
            mine, theirs = choose(
                pieces, z * (plane * NC), core, at_facts + 1, NC * rows, block
            )
            theirs = shift(theirs, "c", 1)
        if k == 2:
            lanes = mine.shape[1] // NEWMAX
            early = jnp.where(core == 0, mine, theirs)
            late = jnp.where(core == 0, theirs, mine)
            early = [early[:, n * lanes : (n + 1) * lanes] for n in range(NEWMAX)]
            late = [late[:, n * lanes : (n + 1) * lanes] for n in range(NEWMAX)]
            taken = [e[:, at_facts : at_facts + 1] > 0 for e in early]
            second = jnp.where(taken[0], late[0], late[1])
            bound = jnp.concatenate(
                [jnp.where(taken[0], early[0], late[0]), jnp.where(taken[1], early[1], second)],
                axis=1,
            )
            bound, *_ = tie(bound, *lead)
            bound = lax.ppermute(bound, "g", [(0, 1)])
    total = [
        of(part0, 0) + lead_got[0].astype(f32) + back_got[1].astype(f32),
        of(part0, 1) + back_got[0].astype(f32) + lead_got[1].astype(f32),
    ]
    total = jnp.concatenate(total).astype(bf16)
    total = jnp.concatenate([total, bound], axis=1)
    total = lax.all_to_all(total, ("x", "y"), split_axis=0, concat_axis=0, tiled=True)
    got = total[:, half:]
    total = jnp.sum(total[:, :half].reshape(plane, NC * rows, half).astype(f32), axis=0)
    total = total.astype(bf16)
    mine = lax.dynamic_slice_in_dim(total, core * rows, rows, 0)
    other = shift(lax.dynamic_slice_in_dim(total, (1 - core) * rows, rows, 0), "c", 1)
    expert_out = in_order(mine, other, 1)

    got = got.reshape(plane, 2, rows, NEWMAX, -1)
    pages = jnp.concatenate([got[:, 0, :, :, :wide], got[:, 1, :, :, :wide]], axis=-1)
    pages = jnp.transpose(pages, (2, 0, 1, 3)).reshape(NEWMAX, new_len, latent_width)
    facts = got[0, 0, 0, :, at_facts : at_facts + 3].astype(jnp.int32)
    fresh = attend_new(
        queries[:NEWMAX], query_ids[:NEWMAX], pages, facts[:, 2] - 1, facts[:, 0]
    ).astype(bf16)
    fresh = jnp.where(query_ids[:NEWMAX, None, None] >= RES, fresh, mixed[:NEWMAX])
    attention = jnp.concatenate([fresh, mixed[NEWMAX:]])
    return (expert_out, attention)


def solution(mesh):
    fine = Mesh(mesh.devices.reshape(2, NZ, NX, NY, NC), ALL)
    placed = (
        P(ALL, None),
        P(ALL, None),
        P(ALL, None),
        P(None, EP),
        P(None, EP),
        P(EP, None),
        P(ALL, None, None),
        P(ALL),
        P(ALL, None),
        P(ALL),
        P(ALL, None),
        P(ALL),
        P(ALL),
    )
    return jax.shard_map(
        shards,
        mesh=fine,
        in_specs=placed,
        out_specs=(P(ALL, None), P(ALL, None, None)),
        check_vma=False,
    )
```

```python
import jax
import jax.numpy as jnp
from jax import lax
from jax.experimental import pallas as pl
from jax.experimental.pallas import tpu as pltpu
from jax.sharding import Mesh, PartitionSpec as P

EXPERTS = 16
KVR = 512
RES = 4
NEWMAX = 2
NZ, NX, NY, NC = 8, 4, 2, 2
EP = ("z", "x", "y", "c")
ALL = ("g",) + EP

score_scale = 192.0 ** (-0.5)


def shift(value, axis, by):
    length = lax.axis_size(axis)
    return lax.ppermute(value, axis, [(i, (i + by) % length) for i in range(length)])


def tie(*values):
    return lax.optimization_barrier(values)


def cached_kernel(ids_ref, owner_ref, q_ref, pool_ref, out_ref, score_ref):
    rows, _, heads = q_ref.shape
    keys = pool_ref.shape[1]
    step, lanes = 512, 128
    columns = [slice(n * lanes, (n + 1) * lanes) for n in range(step // lanes)]
    blocks = [slice(n, n + step) for n in range(0, keys, step)]
    queries = jnp.concatenate([q_ref[r] for r in range(rows)], axis=1).T
    tops = [jnp.full((heads, lanes), -jnp.inf, jnp.float32) for _ in range(rows)]
    for at in blocks:
        scores = jnp.dot(queries, pool_ref[:, at], preferred_element_type=jnp.float32)
        for r in range(rows):
            part = scores[r * heads : (r + 1) * heads] * score_scale
            part = jnp.where(owner_ref[:, at] == ids_ref[r], part, -jnp.inf)
            score_ref[r, :, at] = part
            for column in columns:
                tops[r] = jnp.maximum(tops[r], part[:, column])
    inverse = []
    for r in range(rows):
        top = jnp.maximum(jnp.max(tops[r], axis=1, keepdims=True), -3e38)
        total = jnp.zeros((heads, lanes), jnp.float32)
        for at in blocks:
            part = jnp.exp(score_ref[r, :, at] - top)
            score_ref[r, :, at] = part
            for column in columns:
                total = total + part[:, column]
        inverse.append(1.0 / jnp.maximum(jnp.sum(total, axis=1, keepdims=True), 1e-30))
    mixed = jnp.zeros((rows * heads, KVR), jnp.float32)
    for at in blocks:
        probs = [(score_ref[r, :, at] * inverse[r]).astype(jnp.bfloat16) for r in range(rows)]
        mixed = mixed + lax.dot_general(
            jnp.concatenate(probs),
            pool_ref[:KVR, at],
            (((1,), (1,)), ((), ())),
            preferred_element_type=jnp.float32,
        )
    out_ref[...] = mixed.reshape(out_ref.shape).astype(out_ref.dtype)


def attend_cached(queries, query_ids, latent_pool, key_owner):
    rows, heads, latent = queries.shape
    keys = latent_pool.shape[0]
    return pl.pallas_call(
        cached_kernel,
        out_shape=jax.ShapeDtypeStruct((rows, heads, KVR), jnp.bfloat16),
        in_specs=[pl.BlockSpec(memory_space=pltpu.SMEM)]
        + [pl.BlockSpec(memory_space=pltpu.VMEM)] * 3,
        out_specs=pl.BlockSpec(memory_space=pltpu.VMEM),
        scratch_shapes=[pltpu.VMEM((rows, heads, keys), jnp.float32)],
        compiler_params=pltpu.CompilerParams(vmem_limit_bytes=20 << 20),
        cost_estimate=pl.CostEstimate(
            flops=2 * rows * heads * keys * (latent + KVR),
            bytes_accessed=2 * keys * latent,
            transcendentals=rows * heads * keys,
        ),
    )(query_ids, key_owner.reshape(1, keys), jnp.swapaxes(queries, 1, 2), latent_pool.T)


def choose_kernel(at_ref, rank_lane, group, pieces_ref, mine_ref, their_ref):
    bf16, f32, i32 = jnp.bfloat16, jnp.float32, jnp.int32
    pieces = pieces_ref[...]
    count, lanes = pieces.shape
    sources = count // group
    rows = mine_ref.shape[0]

    def iota(shape, axis):
        return lax.broadcasted_iota(i32, shape, axis)

    pick = iota((sources, count), 1) == iota((sources, count), 0) * group
    facts = jnp.dot(pick.astype(bf16), pieces, preferred_element_type=f32)
    lane = (iota((8, lanes), 1) == rank_lane).astype(bf16)
    along = lax.dot_general(
        lane, facts.astype(bf16), (((1,), (1,)), ((), ())), preferred_element_type=f32
    )
    down = facts[:, rank_lane : rank_lane + 1]
    earlier = iota((sources, sources), 0) < iota((sources, sources), 1)
    turn = jnp.where((down == along[:1]) & earlier, 1.0, 0.0)
    turn = jnp.sum(turn, axis=0, keepdims=True)
    repeat = (iota((sources, count), 1) // group == iota((sources, count), 0)).astype(bf16)
    along = jnp.dot(along.astype(bf16), repeat, preferred_element_type=f32)[:1].astype(i32)
    turn = jnp.broadcast_to(turn, (8, sources)).astype(bf16)
    turn = jnp.dot(turn, repeat, preferred_element_type=f32)[:1].astype(i32)
    row, column = iota((rows, count), 0), iota((rows, count), 1)
    aligned = row % group == column % group
    for side, target in ((at_ref[1], mine_ref), (1 - at_ref[1], their_ref)):
        here = at_ref[0] + row // group * NC + side
        for slot in range(NEWMAX):
            chosen = aligned & (along == here) & (turn == slot)
            target[:, slot * lanes : (slot + 1) * lanes] = jnp.dot(
                chosen.astype(bf16), pieces, preferred_element_type=f32
            ).astype(bf16)


def choose(pieces, first, core, rank_lane, group, rows):
    shape = jax.ShapeDtypeStruct((rows, NEWMAX * pieces.shape[1]), jnp.bfloat16)
    vmem = pl.BlockSpec(memory_space=pltpu.VMEM)

    def kernel(at_ref, pieces_ref, mine_ref, their_ref):
        choose_kernel(at_ref, rank_lane, group, pieces_ref, mine_ref, their_ref)

    return pl.pallas_call(
        kernel,
        out_shape=(shape, shape),
        in_specs=[pl.BlockSpec(memory_space=pltpu.SMEM), vmem],
        out_specs=(vmem, vmem),
        compiler_params=pltpu.CompilerParams(vmem_limit_bytes=8 << 20),
        cost_estimate=pl.CostEstimate(
            flops=8 * pieces.size * rows, bytes_accessed=4 * pieces.size, transcendentals=0
        ),
    )(jnp.stack([first, core]), pieces)


def fresh_kernel(at_facts, ids_ref, got_ref, q_ref, mixed_ref, out_ref):
    bf16, f32 = jnp.bfloat16, jnp.float32
    rows, latent, heads = q_ref.shape
    count = got_ref.shape[0]
    lanes, wide, keys = got_ref.shape[1] // NEWMAX, latent // 2, count // 2

    def iota(shape, axis):
        return lax.broadcasted_iota(jnp.int32, shape, axis)

    row, column = iota((keys, count), 0), iota((keys, count), 1)
    start = row // 4 * 8 + row % 4
    picks = [(column == start + 4 * n).astype(bf16) for n in range(2)]
    pages, lengths, names = [], [], []
    for slot in range(NEWMAX):
        got = got_ref[:, slot * lanes : (slot + 1) * lanes]
        parts = [jnp.dot(pick, got, preferred_element_type=f32) for pick in picks]
        pages.append(jnp.concatenate([part[:, :wide] for part in parts], axis=1))
        facts = got[:16].astype(f32)
        lengths.append(facts[:1, at_facts : at_facts + 1])
        names.append(facts[:1, at_facts + 2 : at_facts + 3])
    for r in range(rows):
        if r >= NEWMAX:
            out_ref[r] = mixed_ref[r]
            continue
        wanted = (ids_ref[r] - RES + 1).astype(f32)
        page = jnp.zeros((keys, latent), f32)
        length = jnp.zeros((1, 1), f32)
        for slot in range(NEWMAX):
            match = names[slot] == wanted
            page = page + jnp.where(match, pages[slot], 0.0)
            length = length + jnp.where(match, lengths[slot], 0.0)
        page = page.astype(bf16)
        scores = jnp.dot(page, q_ref[r], preferred_element_type=f32) * score_scale
        valid = iota((keys, heads), 0).astype(f32) < length
        scores = jnp.where(valid, scores, -jnp.inf)
        best = jnp.maximum(jnp.max(scores, axis=0, keepdims=True), -3e38)
        part = jnp.exp(scores - best)
        total = jnp.maximum(jnp.sum(part, axis=0, keepdims=True), 1e-30)
        probs = (part / total).astype(bf16)
        mixed = lax.dot_general(
            probs, page[:, :KVR], (((0,), (0,)), ((), ())), preferred_element_type=f32
        )
        keep = jnp.where(ids_ref[r] >= RES, 1, 0)
        keep = jnp.full(mixed.shape, keep, jnp.int32) > 0
        out_ref[r] = jnp.where(keep, mixed.astype(f32), mixed_ref[r].astype(f32)).astype(bf16)


def attend_fresh(queries, query_ids, got, mixed, at_facts):
    vmem = pl.BlockSpec(memory_space=pltpu.VMEM)

    def kernel(*refs):
        fresh_kernel(at_facts, *refs)

    return pl.pallas_call(
        kernel,
        out_shape=jax.ShapeDtypeStruct(mixed.shape, mixed.dtype),
        in_specs=[pl.BlockSpec(memory_space=pltpu.SMEM)] + [vmem] * 3,
        out_specs=vmem,
        compiler_params=pltpu.CompilerParams(vmem_limit_bytes=12 << 20),
        cost_estimate=pl.CostEstimate(
            flops=1 << 27, bytes_accessed=4 * mixed.size, transcendentals=1 << 13
        ),
    )(query_ids, got, jnp.swapaxes(queries, 1, 2), mixed)


def shards(
    rows_in,
    expert_ids,
    gate_values,
    w_gate,
    w_up,
    w_down,
    queries,
    query_ids,
    latent_pool,
    key_owner,
    sent_pages,
    sent_length,
    sent_rank,
):
    bf16, f32 = jnp.bfloat16, jnp.float32
    rows, width = rows_in.shape
    half = width // NC
    z, core = lax.axis_index("z"), lax.axis_index("c")
    place = lax.axis_index(("z", "x", "y", "c"))
    rank_count = NZ * NX * NY * NC
    plane = NX * NY
    block = plane * NC * rows
    new_len, latent_width = sent_pages.shape
    hid = w_gate.shape[1]

    def halves(value, axis):
        size = value.shape[axis] // NC
        mine = lax.dynamic_slice_in_dim(value, core * size, size, axis)
        theirs = lax.dynamic_slice_in_dim(value, (1 - core) * size, size, axis)
        return mine, shift(theirs, "c", 1)

    def in_order(mine, other, axis):
        return jnp.where(
            core == 0,
            jnp.concatenate([mine, other], axis=axis),
            jnp.concatenate([other, mine], axis=axis),
        )

    mine, other = halves(rows_in, 1)
    expert_iota = jnp.arange(EXPERTS, dtype=jnp.int32)
    matches = expert_ids[:, :, None] == expert_iota[None, None]
    weight = jnp.sum(jnp.where(matches, gate_values[:, :, None], 0), axis=1, dtype=bf16)
    expert_iota = expert_iota[None]
    chip_rows = in_order(mine, other, 0)
    chip_weight = in_order(weight, shift(weight, "c", 1), 0)

    wide = latent_width // 2
    piece = jnp.concatenate(
        [sent_pages[:, n * wide : (n + 1) * wide].reshape(plane, -1, wide) for n in range(2)],
        axis=1,
    )
    facts = jnp.concatenate([sent_length, sent_rank, place[None] + 1]).astype(bf16)
    facts = jnp.broadcast_to(facts[None, None], (plane, NC * rows, 3))
    spread = jnp.concatenate(
        [
            jnp.broadcast_to(chip_rows[None], (plane,) + chip_rows.shape),
            piece,
            jnp.broadcast_to(chip_weight[None], (plane,) + chip_weight.shape),
            facts,
        ],
        axis=2,
    )
    used = spread.shape[2]
    spread = jnp.pad(spread, ((0, 0), (0, 0), (0, -used % 128))).reshape(block, -1)
    at_weight = half + wide
    at_facts = at_weight + EXPERTS - half

    spread, ids = tie(spread, query_ids)
    own = lax.all_to_all(spread, ("x", "y"), split_axis=0, concat_axis=0, tiled=True)

    mixed = attend_cached(queries, ids, latent_pool, key_owner)
    own, mixed, w_gate, w_up, w_down = tie(own, mixed, w_gate, w_up, w_down)

    gate_mine, gate_other = halves(w_gate, 0)
    up_mine, up_other = halves(w_up, 0)
    down_mine, down_other = halves(w_down, 1)
    expert = z * (EXPERTS // NZ) + lax.axis_index("x") // (NX * NZ // EXPERTS)

    def enter(*data):
        data = jnp.concatenate(data)
        proj = jnp.dot(data[:, :half], w_in, preferred_element_type=f32)
        scale = jnp.sum(
            jnp.where(
                expert_iota == expert, data[:, at_weight : at_weight + EXPERTS].astype(f32), 0.0
            ),
            axis=1,
            keepdims=True,
        )
        return proj, scale, shift(proj, "c", 1)

    def leave(proj, scale, came):
        swapped = jnp.concatenate(
            [came[:, hid : 2 * hid], came[:, :hid], came[:, 3 * hid :], came[:, 2 * hid : 3 * hid]],
            axis=1,
        )
        proj = proj + swapped
        hidden = (jax.nn.silu(proj[:, : 2 * hid]) * proj[:, 2 * hid :]).astype(bf16)
        return jnp.dot(hidden, w_out, preferred_element_type=f32) * scale

    def send(pair):
        return shift(pair[0], "z", 1), shift(pair[1], "z", -1)

    def after(pair, *others):
        tied = tie(*pair, *others)
        return tied[:2], *tied[2:]

    rest = block // 2
    top, low = own[:rest], own[rest:]
    lead, back = (top, low), (low, top)
    lead1 = send(lead)
    back, gate_mine, up_mine, down_mine = after(back, gate_mine, up_mine, down_mine)
    back1 = send(back)
    w_in = jnp.concatenate([gate_mine, gate_other, up_mine, up_other], axis=1)
    w_out = jnp.concatenate([down_mine, down_other], axis=0)
    lead1, w_in, w_out, *_ = after(lead1, w_in, w_out, *back)
    lead2 = send(lead1)
    back1, *_ = after(back1, *lead1)
    back2 = send(back1)
    proj0, scale0, came0 = enter(top, low, *lead1, *back1)
    lead2, proj0, scale0, *_ = after(lead2, proj0, scale0, *back1)
    lead3 = send(lead2)
    back2, came0, *_ = after(back2, came0, *lead2)
    back3 = send(back2)
    proj2, scale2, came2 = enter(*lead2, *back2)
    part0 = leave(proj0, scale0, came0)
    lead3, proj2, scale2, part0, *_ = after(lead3, proj2, scale2, part0, *back2)
    lead4 = send(lead3)
    back3, came2, *_ = after(back3, came2, *lead3)
    proj3, scale3, came3 = enter(*lead3, *back3)
    part2 = leave(proj2, scale2, came2)
    lead4, proj3, scale3, part2 = after(lead4, proj3, scale3, part2)
    proj4, scale4, came4 = enter(*lead4)
    proj4, came3 = tie(proj4, came3)
    part3 = leave(proj3, scale3, came3)
    part4 = leave(proj4, scale4, came4)

    def of(part, n):
        return part[n * rest : (n + 1) * rest]

    def add(got, mine, first, second):
        part, offset = mine
        pair = zip(got, (of(part, offset + first), of(part, offset + second)))
        return tie(*((g.astype(f32) + p).astype(bf16) for g, p in pair))

    lead = tie(of(part4, 0).astype(bf16), of(part4, 1).astype(bf16))
    back = tie(of(part3, 1).astype(bf16), of(part3, 0).astype(bf16))
    parts = {3: (part3, 0), 2: (part2, 0), 1: (part0, 2)}
    pieces = (own, *lead1, *back1, *lead2, *back2, *lead3, *back3, *lead4)
    pieces = jnp.concatenate([p[:, half:] for p in pieces])
    lead_got, back_got = send(lead), send(back)
    for k in (3, 2, 1):
        lead_got, *_ = after(lead_got, *back)
        if k == 1:
            lead_got, bound = after(lead_got, bound)
        lead = add(lead_got, parts[k], 3, 2)
        lead_got = send(lead)
        if k > 1:
            back_got, *_ = after(back_got, *lead)
            back = add(back_got, parts[k - 1], 1, 0)
            back_got = send(back)
        if k == 3:
            pieces, *_ = tie(pieces, *lead)
            mine, theirs = choose(
                pieces, z * (plane * NC), core, at_facts + 1, NC * rows, block
            )
            theirs = shift(theirs, "c", 1)
        if k == 2:
            lanes = mine.shape[1] // NEWMAX
            early = jnp.where(core == 0, mine, theirs)
            late = jnp.where(core == 0, theirs, mine)
            early = [early[:, n * lanes : (n + 1) * lanes] for n in range(NEWMAX)]
            late = [late[:, n * lanes : (n + 1) * lanes] for n in range(NEWMAX)]
            taken = [e[:, at_facts : at_facts + 1] > 0 for e in early]
            second = jnp.where(taken[0], late[0], late[1])
            bound = jnp.concatenate(
                [jnp.where(taken[0], early[0], late[0]), jnp.where(taken[1], early[1], second)],
                axis=1,
            )
            bound, *_ = tie(bound, *lead)
            bound = lax.ppermute(bound, "g", [(0, 1)])
    total = [
        of(part0, 0) + lead_got[0].astype(f32) + back_got[1].astype(f32),
        of(part0, 1) + back_got[0].astype(f32) + lead_got[1].astype(f32),
    ]
    total = jnp.concatenate(total).astype(bf16)
    total = jnp.concatenate([total, bound], axis=1)
    total = lax.all_to_all(total, ("x", "y"), split_axis=0, concat_axis=0, tiled=True)
    got = total[:, half:]
    total = jnp.sum(total[:, :half].reshape(plane, NC * rows, half).astype(f32), axis=0)
    total = total.astype(bf16)
    mine = lax.dynamic_slice_in_dim(total, core * rows, rows, 0)
    other = shift(lax.dynamic_slice_in_dim(total, (1 - core) * rows, rows, 0), "c", 1)
    expert_out = in_order(mine, other, 1)

    attention = attend_fresh(queries, query_ids, got, mixed, at_facts)
    return (expert_out, attention)


def solution(mesh):
    fine = Mesh(mesh.devices.reshape(2, NZ, NX, NY, NC), ALL)
    placed = (
        P(ALL, None),
        P(ALL, None),
        P(ALL, None),
        P(None, EP),
        P(None, EP),
        P(EP, None),
        P(ALL, None, None),
        P(ALL),
        P(ALL, None),
        P(ALL),
        P(ALL, None),
        P(ALL),
        P(ALL),
    )
    return jax.shard_map(
        shards,
        mesh=fine,
        in_specs=placed,
        out_specs=(P(ALL, None), P(ALL, None, None)),
        check_vma=False,
    )
```

```python
import jax
import jax.numpy as jnp
from jax import lax
from jax.experimental import pallas as pl
from jax.experimental.pallas import tpu as pltpu
from jax.sharding import Mesh, PartitionSpec as P

EXPERTS = 16
KVR = 512
RES = 4
NEWMAX = 2
NZ, NX, NY, NC = 8, 4, 2, 2
EP = ("z", "x", "y", "c")
ALL = ("g",) + EP

score_scale = 192.0 ** (-0.5)


def shift(value, axis, by):
    length = lax.axis_size(axis)
    return lax.ppermute(value, axis, [(i, (i + by) % length) for i in range(length)])


def tie(*values):
    return lax.optimization_barrier(values)


def cached_kernel(ids_ref, owner_ref, q_ref, pool_ref, out_ref, score_ref):
    rows, _, heads = q_ref.shape
    keys = pool_ref.shape[1]
    step, lanes = 1024, 128
    columns = [slice(n * lanes, (n + 1) * lanes) for n in range(step // lanes)]
    blocks = [slice(n, n + step) for n in range(0, keys, step)]
    queries = jnp.concatenate([q_ref[r] for r in range(rows)], axis=1).T
    tops = [jnp.full((heads, lanes), -jnp.inf, jnp.float32) for _ in range(rows)]
    for at in blocks:
        scores = jnp.dot(queries, pool_ref[:, at], preferred_element_type=jnp.float32)
        for r in range(rows):
            part = scores[r * heads : (r + 1) * heads] * score_scale
            part = jnp.where(owner_ref[:, at] == ids_ref[r], part, -jnp.inf)
            score_ref[r, :, at] = part
            for column in columns:
                tops[r] = jnp.maximum(tops[r], part[:, column])
    inverse = []
    for r in range(rows):
        top = jnp.maximum(jnp.max(tops[r], axis=1, keepdims=True), -3e38)
        total = jnp.zeros((heads, lanes), jnp.float32)
        for at in blocks:
            part = jnp.exp(score_ref[r, :, at] - top)
            score_ref[r, :, at] = part
            for column in columns:
                total = total + part[:, column]
        inverse.append(1.0 / jnp.maximum(jnp.sum(total, axis=1, keepdims=True), 1e-30))
    mixed = jnp.zeros((rows * heads, KVR), jnp.float32)
    for at in blocks:
        probs = [(score_ref[r, :, at] * inverse[r]).astype(jnp.bfloat16) for r in range(rows)]
        mixed = mixed + lax.dot_general(
            jnp.concatenate(probs),
            pool_ref[:KVR, at],
            (((1,), (1,)), ((), ())),
            preferred_element_type=jnp.float32,
        )
    out_ref[...] = mixed.reshape(out_ref.shape).astype(out_ref.dtype)


def attend_cached(queries, query_ids, latent_pool, key_owner):
    rows, heads, latent = queries.shape
    keys = latent_pool.shape[0]
    return pl.pallas_call(
        cached_kernel,
        out_shape=jax.ShapeDtypeStruct((rows, heads, KVR), jnp.bfloat16),
        in_specs=[pl.BlockSpec(memory_space=pltpu.SMEM)]
        + [pl.BlockSpec(memory_space=pltpu.VMEM)] * 3,
        out_specs=pl.BlockSpec(memory_space=pltpu.VMEM),
        scratch_shapes=[pltpu.VMEM((rows, heads, keys), jnp.float32)],
        compiler_params=pltpu.CompilerParams(vmem_limit_bytes=20 << 20),
        cost_estimate=pl.CostEstimate(
            flops=2 * rows * heads * keys * (latent + KVR),
            bytes_accessed=2 * keys * latent,
            transcendentals=rows * heads * keys,
        ),
    )(query_ids, key_owner.reshape(1, keys), jnp.swapaxes(queries, 1, 2), latent_pool.T)


def choose_kernel(at_ref, rank_lane, group, pieces_ref, mine_ref, their_ref):
    bf16, f32, i32 = jnp.bfloat16, jnp.float32, jnp.int32
    pieces = pieces_ref[...]
    count, lanes = pieces.shape
    sources = count // group
    rows = mine_ref.shape[0]

    def iota(shape, axis):
        return lax.broadcasted_iota(i32, shape, axis)

    pick = iota((sources, count), 1) == iota((sources, count), 0) * group
    facts = jnp.dot(pick.astype(bf16), pieces, preferred_element_type=f32)
    lane = (iota((8, lanes), 1) == rank_lane).astype(bf16)
    along = lax.dot_general(
        lane, facts.astype(bf16), (((1,), (1,)), ((), ())), preferred_element_type=f32
    )
    down = facts[:, rank_lane : rank_lane + 1]
    earlier = iota((sources, sources), 0) < iota((sources, sources), 1)
    turn = jnp.where((down == along[:1]) & earlier, 1.0, 0.0)
    turn = jnp.sum(turn, axis=0, keepdims=True)
    repeat = (iota((sources, count), 1) // group == iota((sources, count), 0)).astype(bf16)
    along = jnp.dot(along.astype(bf16), repeat, preferred_element_type=f32)[:1].astype(i32)
    turn = jnp.broadcast_to(turn, (8, sources)).astype(bf16)
    turn = jnp.dot(turn, repeat, preferred_element_type=f32)[:1].astype(i32)
    row, column = iota((rows, count), 0), iota((rows, count), 1)
    aligned = row % group == column % group
    for side, target in ((at_ref[1], mine_ref), (1 - at_ref[1], their_ref)):
        here = at_ref[0] + row // group * NC + side
        for slot in range(NEWMAX):
            chosen = aligned & (along == here) & (turn == slot)
            target[:, slot * lanes : (slot + 1) * lanes] = jnp.dot(
                chosen.astype(bf16), pieces, preferred_element_type=f32
            ).astype(bf16)


def choose(pieces, first, core, rank_lane, group, rows):
    shape = jax.ShapeDtypeStruct((rows, NEWMAX * pieces.shape[1]), jnp.bfloat16)
    vmem = pl.BlockSpec(memory_space=pltpu.VMEM)

    def kernel(at_ref, pieces_ref, mine_ref, their_ref):
        choose_kernel(at_ref, rank_lane, group, pieces_ref, mine_ref, their_ref)

    return pl.pallas_call(
        kernel,
        out_shape=(shape, shape),
        in_specs=[pl.BlockSpec(memory_space=pltpu.SMEM), vmem],
        out_specs=(vmem, vmem),
        compiler_params=pltpu.CompilerParams(vmem_limit_bytes=8 << 20),
        cost_estimate=pl.CostEstimate(
            flops=8 * pieces.size * rows, bytes_accessed=4 * pieces.size, transcendentals=0
        ),
    )(jnp.stack([first, core]), pieces)


def fresh_kernel(at_facts, ids_ref, got_ref, q_ref, mixed_ref, out_ref):
    bf16, f32 = jnp.bfloat16, jnp.float32
    rows, latent, heads = q_ref.shape
    count = got_ref.shape[0]
    lanes, wide, keys = got_ref.shape[1] // NEWMAX, latent // 2, count // 2

    def iota(shape, axis):
        return lax.broadcasted_iota(jnp.int32, shape, axis)

    row, column = iota((keys, count), 0), iota((keys, count), 1)
    start = row // 4 * 8 + row % 4
    picks = [(column == start + 4 * n).astype(bf16) for n in range(2)]
    pages, lengths, names = [], [], []
    for slot in range(NEWMAX):
        got = got_ref[:, slot * lanes : (slot + 1) * lanes]
        parts = [jnp.dot(pick, got, preferred_element_type=f32) for pick in picks]
        pages.append(jnp.concatenate([part[:, :wide] for part in parts], axis=1))
        facts = got[:16].astype(f32)
        lengths.append(facts[:1, at_facts : at_facts + 1])
        names.append(facts[:1, at_facts + 2 : at_facts + 3])
    for r in range(rows):
        if r >= NEWMAX:
            out_ref[r] = mixed_ref[r]
            continue
        wanted = (ids_ref[r] - RES + 1).astype(f32)
        page = jnp.zeros((keys, latent), f32)
        length = jnp.zeros((1, 1), f32)
        for slot in range(NEWMAX):
            match = names[slot] == wanted
            page = page + jnp.where(match, pages[slot], 0.0)
            length = length + jnp.where(match, lengths[slot], 0.0)
        page = page.astype(bf16)
        scores = jnp.dot(page, q_ref[r], preferred_element_type=f32) * score_scale
        valid = iota((keys, heads), 0).astype(f32) < length
        scores = jnp.where(valid, scores, -jnp.inf)
        best = jnp.maximum(jnp.max(scores, axis=0, keepdims=True), -3e38)
        part = jnp.exp(scores - best)
        total = jnp.maximum(jnp.sum(part, axis=0, keepdims=True), 1e-30)
        probs = (part / total).astype(bf16)
        mixed = lax.dot_general(
            probs, page[:, :KVR], (((0,), (0,)), ((), ())), preferred_element_type=f32
        )
        keep = jnp.where(ids_ref[r] >= RES, 1, 0)
        keep = jnp.full(mixed.shape, keep, jnp.int32) > 0
        out_ref[r] = jnp.where(keep, mixed.astype(f32), mixed_ref[r].astype(f32)).astype(bf16)


def attend_fresh(queries, query_ids, got, mixed, at_facts):
    vmem = pl.BlockSpec(memory_space=pltpu.VMEM)

    def kernel(*refs):
        fresh_kernel(at_facts, *refs)

    return pl.pallas_call(
        kernel,
        out_shape=jax.ShapeDtypeStruct(mixed.shape, mixed.dtype),
        in_specs=[pl.BlockSpec(memory_space=pltpu.SMEM)] + [vmem] * 3,
        out_specs=vmem,
        compiler_params=pltpu.CompilerParams(vmem_limit_bytes=12 << 20),
        cost_estimate=pl.CostEstimate(
            flops=1 << 27, bytes_accessed=4 * mixed.size, transcendentals=1 << 13
        ),
    )(query_ids, got, jnp.swapaxes(queries, 1, 2), mixed)


def shards(
    rows_in,
    expert_ids,
    gate_values,
    w_gate,
    w_up,
    w_down,
    queries,
    query_ids,
    latent_pool,
    key_owner,
    sent_pages,
    sent_length,
    sent_rank,
):
    bf16, f32 = jnp.bfloat16, jnp.float32
    rows, width = rows_in.shape
    half = width // NC
    z, core = lax.axis_index("z"), lax.axis_index("c")
    place = lax.axis_index(("z", "x", "y", "c"))
    rank_count = NZ * NX * NY * NC
    plane = NX * NY
    block = plane * NC * rows
    new_len, latent_width = sent_pages.shape
    hid = w_gate.shape[1]

    def halves(value, axis):
        size = value.shape[axis] // NC
        mine = lax.dynamic_slice_in_dim(value, core * size, size, axis)
        theirs = lax.dynamic_slice_in_dim(value, (1 - core) * size, size, axis)
        return mine, shift(theirs, "c", 1)

    def in_order(mine, other, axis):
        return jnp.where(
            core == 0,
            jnp.concatenate([mine, other], axis=axis),
            jnp.concatenate([other, mine], axis=axis),
        )

    mine, other = halves(rows_in, 1)
    expert_iota = jnp.arange(EXPERTS, dtype=jnp.int32)
    matches = expert_ids[:, :, None] == expert_iota[None, None]
    weight = jnp.sum(jnp.where(matches, gate_values[:, :, None], 0), axis=1, dtype=bf16)
    expert_iota = expert_iota[None]
    chip_rows = in_order(mine, other, 0)
    chip_weight = in_order(weight, shift(weight, "c", 1), 0)

    wide = latent_width // 2
    piece = jnp.concatenate(
        [sent_pages[:, n * wide : (n + 1) * wide].reshape(plane, -1, wide) for n in range(2)],
        axis=1,
    )
    facts = jnp.concatenate([sent_length, sent_rank, place[None] + 1]).astype(bf16)
    facts = jnp.broadcast_to(facts[None, None], (plane, NC * rows, 3))
    spread = jnp.concatenate(
        [
            jnp.broadcast_to(chip_rows[None], (plane,) + chip_rows.shape),
            piece,
            jnp.broadcast_to(chip_weight[None], (plane,) + chip_weight.shape),
            facts,
        ],
        axis=2,
    )
    used = spread.shape[2]
    spread = jnp.pad(spread, ((0, 0), (0, 0), (0, -used % 128))).reshape(block, -1)
    at_weight = half + wide
    at_facts = at_weight + EXPERTS - half

    spread, ids = tie(spread, query_ids)
    own = lax.all_to_all(spread, ("x", "y"), split_axis=0, concat_axis=0, tiled=True)

    mixed = attend_cached(queries, ids, latent_pool, key_owner)
    own, mixed, w_gate, w_up, w_down = tie(own, mixed, w_gate, w_up, w_down)

    gate_mine, gate_other = halves(w_gate, 0)
    up_mine, up_other = halves(w_up, 0)
    down_mine, down_other = halves(w_down, 1)
    expert = z * (EXPERTS // NZ) + lax.axis_index("x") // (NX * NZ // EXPERTS)

    def enter(*data):
        data = jnp.concatenate(data)
        proj = jnp.dot(data[:, :half], w_in, preferred_element_type=f32)
        scale = jnp.sum(
            jnp.where(
                expert_iota == expert, data[:, at_weight : at_weight + EXPERTS].astype(f32), 0.0
            ),
            axis=1,
            keepdims=True,
        )
        return proj, scale, shift(proj, "c", 1)

    def leave(proj, scale, came):
        swapped = jnp.concatenate(
            [came[:, hid : 2 * hid], came[:, :hid], came[:, 3 * hid :], came[:, 2 * hid : 3 * hid]],
            axis=1,
        )
        proj = proj + swapped
        hidden = (jax.nn.silu(proj[:, : 2 * hid]) * proj[:, 2 * hid :]).astype(bf16)
        return jnp.dot(hidden, w_out, preferred_element_type=f32) * scale

    def send(pair):
        return shift(pair[0], "z", 1), shift(pair[1], "z", -1)

    def after(pair, *others):
        tied = tie(*pair, *others)
        return tied[:2], *tied[2:]

    rest = block // 2
    top, low = own[:rest], own[rest:]
    lead, back = (top, low), (low, top)
    lead1 = send(lead)
    back, gate_mine, up_mine, down_mine = after(back, gate_mine, up_mine, down_mine)
    back1 = send(back)
    w_in = jnp.concatenate([gate_mine, gate_other, up_mine, up_other], axis=1)
    w_out = jnp.concatenate([down_mine, down_other], axis=0)
    lead1, w_in, w_out, *_ = after(lead1, w_in, w_out, *back)
    lead2 = send(lead1)
    back1, *_ = after(back1, *lead1)
    back2 = send(back1)
    proj0, scale0, came0 = enter(top, low, *lead1, *back1)
    lead2, proj0, scale0, *_ = after(lead2, proj0, scale0, *back1)
    lead3 = send(lead2)
    back2, came0, *_ = after(back2, came0, *lead2)
    back3 = send(back2)
    proj2, scale2, came2 = enter(*lead2, *back2)
    part0 = leave(proj0, scale0, came0)
    lead3, proj2, scale2, part0, *_ = after(lead3, proj2, scale2, part0, *back2)
    lead4 = send(lead3)
    back3, came2, *_ = after(back3, came2, *lead3)
    proj3, scale3, came3 = enter(*lead3, *back3)
    part2 = leave(proj2, scale2, came2)
    lead4, proj3, scale3, part2 = after(lead4, proj3, scale3, part2)
    proj4, scale4, came4 = enter(*lead4)
    proj4, came3 = tie(proj4, came3)
    part3 = leave(proj3, scale3, came3)
    part4 = leave(proj4, scale4, came4)

    def of(part, n):
        return part[n * rest : (n + 1) * rest]

    def add(got, mine, first, second):
        part, offset = mine
        pair = zip(got, (of(part, offset + first), of(part, offset + second)))
        return tie(*((g.astype(f32) + p).astype(bf16) for g, p in pair))

    lead = tie(of(part4, 0).astype(bf16), of(part4, 1).astype(bf16))
    back = tie(of(part3, 1).astype(bf16), of(part3, 0).astype(bf16))
    parts = {3: (part3, 0), 2: (part2, 0), 1: (part0, 2)}
    pieces = (own, *lead1, *back1, *lead2, *back2, *lead3, *back3, *lead4)
    pieces = jnp.concatenate([p[:, half:] for p in pieces])
    lead_got, back_got = send(lead), send(back)
    for k in (3, 2, 1):
        lead_got, *_ = after(lead_got, *back)
        if k == 1:
            lead_got, bound = after(lead_got, bound)
        lead = add(lead_got, parts[k], 3, 2)
        lead_got = send(lead)
        if k > 1:
            back_got, *_ = after(back_got, *lead)
            back = add(back_got, parts[k - 1], 1, 0)
            back_got = send(back)
        if k == 3:
            pieces, *_ = tie(pieces, *lead)
            mine, theirs = choose(
                pieces, z * (plane * NC), core, at_facts + 1, NC * rows, block
            )
            theirs = shift(theirs, "c", 1)
        if k == 2:
            lanes = mine.shape[1] // NEWMAX
            early = jnp.where(core == 0, mine, theirs)
            late = jnp.where(core == 0, theirs, mine)
            early = [early[:, n * lanes : (n + 1) * lanes] for n in range(NEWMAX)]
            late = [late[:, n * lanes : (n + 1) * lanes] for n in range(NEWMAX)]
            taken = [e[:, at_facts : at_facts + 1] > 0 for e in early]
            second = jnp.where(taken[0], late[0], late[1])
            bound = jnp.concatenate(
                [jnp.where(taken[0], early[0], late[0]), jnp.where(taken[1], early[1], second)],
                axis=1,
            )
            bound, *_ = tie(bound, *lead)
            bound = lax.ppermute(bound, "g", [(0, 1)])
    total = [
        of(part0, 0) + lead_got[0].astype(f32) + back_got[1].astype(f32),
        of(part0, 1) + back_got[0].astype(f32) + lead_got[1].astype(f32),
    ]
    total = jnp.concatenate(total).astype(bf16)
    total = jnp.concatenate([total, bound], axis=1)
    total = lax.all_to_all(total, ("x", "y"), split_axis=0, concat_axis=0, tiled=True)
    got = total[:, half:]
    total = jnp.sum(total[:, :half].reshape(plane, NC * rows, half).astype(f32), axis=0)
    total = total.astype(bf16)
    mine = lax.dynamic_slice_in_dim(total, core * rows, rows, 0)
    other = shift(lax.dynamic_slice_in_dim(total, (1 - core) * rows, rows, 0), "c", 1)
    expert_out = in_order(mine, other, 1)

    attention = attend_fresh(queries, query_ids, got, mixed, at_facts)
    return (expert_out, attention)


def solution(mesh):
    fine = Mesh(mesh.devices.reshape(2, NZ, NX, NY, NC), ALL)
    placed = (
        P(ALL, None),
        P(ALL, None),
        P(ALL, None),
        P(None, EP),
        P(None, EP),
        P(EP, None),
        P(ALL, None, None),
        P(ALL),
        P(ALL, None),
        P(ALL),
        P(ALL, None),
        P(ALL),
        P(ALL),
    )
    return jax.shard_map(
        shards,
        mesh=fine,
        in_specs=placed,
        out_specs=(P(ALL, None), P(ALL, None, None)),
        check_vma=False,
    )
```
